256 devices in a mesh: dp: 32 (over y, x, core), tensor: 8 (over z).
Axes of the slice: x: 4, y: 4, z: 8, core: 2. Of those that a mesh axis runs over, the one named last changes fastest.
Arguments:
- acts: bfloat16 [16384, 8192], P('dp', 'tensor'), may hold values from -6 to 6
- weight: bfloat16 [8192, 5120], P('tensor'), may hold values from -0.09375 to 0.09375
- block_ids: int32 [128], P('dp'), may hold values from 0 to 511
- cached_a: bfloat16 [128, 8192, 64], P('dp', 'tensor'), may hold values from -0.0625 to 0.0625
- cached_b: bfloat16 [128, 64, 5120], P('dp', None, 'tensor'), may hold values from -0.75 to 0.75
- renewed_module_numbers: int32 [64], replicated, may hold values from 0 to 511, as said below
- fresh_a: bfloat16 [64, 8192, 64], P('dp', 'tensor'), may hold values from -0.0625 to 0.0625
- renewed_second_matrices: bfloat16 [64, 64, 5120], P('dp', None, 'tensor'), may hold values from -0.75 to 0.75
Outputs:
- projected: bfloat16 [16384, 5120], P('dp', 'tensor')
The draws below stay inside these ranges and needn't reach their ends.
Inputs may be any that keep to these rules, and one draw needn't show every extreme that they name: `renewed_module_numbers`: the ids are distinct, and each is the id of at least one block.
All inputs are finite; a program needn't handle non-finite values.
Results may differ from the reference program's by a relative error of at most 0.0095.
Values may be sent and summed in bfloat16 or wider, within the bound.
A program may use at most 128 MiB of HBM per device.

```python
import jax
import jax.numpy as jnp
from jax import lax

D = 5120
R = 64
LOWRANK_COUNT = 512
BLOCK = 128
IN = 8192
LAYER_COUNT = 128
ROWS = 16384
NEWEST_COUNT = 64


def adapter_plan(key):
    leading_entry, second, tertiary_entry = jax.random.split(key, 3)
    permuted_order = jax.random.permutation(leading_entry, LOWRANK_COUNT).astype(jnp.int32)
    ranking = jax.random.permutation(second, LAYER_COUNT).astype(jnp.int32)
    remaining_entries = NEWEST_COUNT + jax.random.randint(tertiary_entry, (LAYER_COUNT,), 0, LOWRANK_COUNT - NEWEST_COUNT).astype(jnp.int32)
    chosen = jnp.where(ranking < NEWEST_COUNT, ranking, remaining_entries)
    return (permuted_order[chosen], permuted_order[:NEWEST_COUNT])


def draw_block_ids(key, part):
    return adapter_plan(key)[0]


def draw_renewed_module_numbers(key, part):
    return adapter_plan(key)[1]


def strengthened(array, own_key, source, target, shards_of, factor):
    def block_of(dim):
        return (jnp.arange(array.shape[dim]) // (array.shape[dim] // shards_of)).reshape((-1,) + (1,) * (array.ndim - 1 - dim))

    one_side = jax.random.permutation(own_key, shards_of)[block_of(target)]
    far = (block_of(target) + shards_of // 2) % shards_of
    return jnp.where((block_of(source) == one_side) | (block_of(source) == far), factor * array, array)


def block_scale(key, extent, pieces, low, high):
    factor_of = 1.0
    for axis_at, parts in pieces:
        steps = jax.random.uniform(jax.random.fold_in(jax.random.fold_in(key, 6), axis_at), (parts,), jnp.float32, low / len(pieces), high / len(pieces))
        factor_of = factor_of * jnp.repeat(jnp.exp(steps), extent[axis_at] // parts).reshape((-1,) + (1,) * (len(extent) - 1 - axis_at))
    return factor_of


def centred(stream_key, dims, scale, bound, pieces=(), held_as=jnp.bfloat16):
    factor_of = block_scale(stream_key, dims, pieces, -0.22, 0.18) if pieces else 1.0
    drawn = jax.random.normal(stream_key, dims, jnp.float32) * scale * factor_of
    return jnp.minimum(jnp.maximum(drawn, -bound), bound).astype(held_as)


def gaussian_with(rng, extent, deviation, most, cuts, heavy, kind=jnp.bfloat16):
    array = deviation * jax.random.normal(rng, extent, jnp.float32)
    if cuts:
        array = array * block_scale(rng, extent, cuts, -0.22, 0.18)
    return jnp.clip(strengthened(array, jax.random.fold_in(rng, 3), *heavy), -most, most).astype(kind)


def setup_inputs(seed: int = 0) -> dict:
    key_list = jax.random.split(jax.random.key(seed), 9)
    return {
        "acts": centred(key_list[0], (ROWS, IN), 1.0, 6.0, ((0, 32), (1, 8))),
        "weight": gaussian_with(key_list[1], (IN, D), IN ** -0.5, 0.09375, ((0, 8),), (0, 1, 8, 2.0)),
        "block_ids": draw_block_ids(jax.random.fold_in(key_list[8], 71), 0),
        "cached_a": centred(key_list[3], (LAYER_COUNT, IN, R), IN ** -0.5, 0.0625, ((0, 32), (1, 8))),
        "cached_b": centred(key_list[4], (LAYER_COUNT, R, D), R ** -0.5, 0.75, ((0, 32), (2, 8))),
        "renewed_module_numbers": draw_renewed_module_numbers(jax.random.fold_in(key_list[8], 71), 0),
        "fresh_a": centred(key_list[6], (NEWEST_COUNT, IN, R), IN ** -0.5, 0.0625, ((0, 32), (1, 8))),
        "renewed_second_matrices": centred(key_list[7], (NEWEST_COUNT, R, D), R ** -0.5, 0.75, ((0, 32), (2, 8))),
    }


adapter_scale = 2.0


def reference(acts, weight, block_ids, cached_a, cached_b, renewed_module_numbers, fresh_a, renewed_second_matrices):
    base_product_sum = jnp.dot(acts, weight, preferred_element_type=jnp.float32)
    matches = block_ids[:, None] == renewed_module_numbers[None, :]
    refreshed = jnp.any(matches, axis=1)
    position = jnp.argmax(matches.astype(jnp.int32), axis=1).astype(jnp.int32)

    def per_block(index):
        narrowing_matrix = jnp.where(refreshed[index], fresh_a[position[index]], cached_a[index])
        factor_b = jnp.where(refreshed[index], renewed_second_matrices[position[index]], cached_b[index])
        block_rows = lax.dynamic_slice_in_dim(acts, (index * BLOCK).astype(jnp.int32), BLOCK, 0)
        shrink = jnp.dot(block_rows, narrowing_matrix, preferred_element_type=jnp.float32)
        return jnp.dot(shrink, factor_b.astype(jnp.float32), precision=lax.Precision.HIGHEST)

    expand_factor_up = lax.map(per_block, jnp.arange(LAYER_COUNT, dtype=jnp.int32)).reshape(ROWS, D)
    return (base_product_sum + adapter_scale * expand_factor_up).astype(jnp.bfloat16)
```

```python
import jax
import jax.numpy as jnp
from jax import lax
from jax.experimental import pallas as pl
from jax.experimental.pallas import tpu as pltpu
from jax.sharding import PartitionSpec as P

adapter_scale = 2.0
Z = 8
SIDE = 4
TILE = 128
BF16 = jnp.bfloat16
F32 = jnp.float32

SLOTS = (
    (True, 0, None),
    (False, 1, None),
    (True, 1, 0),
    (False, 2, 1),
    (True, 2, 2),
    (False, 3, 3),
    (True, 3, 4),
)
LAST_LONG, LAST_SHORT = 6, 5

FIRST, SECOND, FIRST_FAR, SECOND_PAIR, SECOND_FAR, OWN_ON, PAIR_ON, FAR_ON = range(8)
ROWS_ACROSS = 16


def dot(a, b):
    return jnp.dot(a, b, preferred_element_type=F32)


def kernel(
    acts_hbm, weight_hbm, ids_hbm, cached_a_hbm, cached_b_hbm, renewed_hbm, fresh_a_hbm, fresh_b_hbm,
    out_hbm,
    acts, weight, ids, renewed, cached_a, cached_b, every_a, every_b,
    outgoing, incoming, total, result, part_out, part_in, shrunk,
    load_sem, weight_sem, fresh_sem, out_sem,
    ring_send, ring_recv, gather_send, gather_recv, part_send, part_recv, shrunk_send, shrunk_recv,
):
    z = lax.axis_index("tensor")
    dp = lax.axis_index("dp")
    core = dp % 2
    x = (dp // 2) % SIDE
    y = dp // (2 * SIDE)
    depth, width = weight.shape[1], weight.shape[2]
    blocks = ids_hbm.shape[0]
    rows = acts.shape[0]
    half = rows // 2
    tiles = half // TILE
    rank = cached_a.shape[1]

    def at_xy(px, py, pc):
        return {"dp": (py * SIDE + px) * 2 + pc}

    def along(axis, step):
        if axis == 0:
            return at_xy((x + step + SIDE) % SIDE, y, core)
        return at_xy(x, (y + step + SIDE) % SIDE, core)

    sibling = at_xy(x, y, 1 - core)

    def weight_load(i):
        column = pl.multiple_of((z + i) % Z * width, 128)
        return pltpu.make_async_copy(weight_hbm.at[:, pl.ds(column, width)], weight.at[i], weight_sem.at[i])

    loads = [
        pltpu.make_async_copy(acts_hbm, acts, load_sem.at[0]),
        pltpu.make_async_copy(cached_a_hbm, cached_a, load_sem.at[1]),
        pltpu.make_async_copy(cached_b_hbm, cached_b, load_sem.at[2]),
        pltpu.make_async_copy(ids_hbm, ids, load_sem.at[3]),
        pltpu.make_async_copy(renewed_hbm, renewed, load_sem.at[4]),
    ]
    mine = (
        (core * SIDE + y) * SIDE + (x % 2) * 2 + x // 2,
        ((2 + core) * SIDE + x) * SIDE + (y % 2) * 2 + y // 2,
    )
    gathers = ((every_a, fresh_a_hbm), (every_b, fresh_b_hbm))
    fresh_loads = [
        [pltpu.make_async_copy(source.at[j], held.at[mine[j]], fresh_sem.at[g, j]) for j in range(2)]
        for g, (held, source) in enumerate(gathers)
    ]

    loads[0].start()
    weight_load(4).start()

    barrier = pltpu.get_barrier_semaphore()
    for i in range(1, Z):
        pl.semaphore_signal(barrier, inc=1, device_id={"tensor": (z + i) % Z}, device_id_type=pl.DeviceIdType.MESH)
    for axis in range(2):
        for step in (1, -1):
            pl.semaphore_signal(barrier, inc=1, device_id=along(axis, step), device_id_type=pl.DeviceIdType.MESH)
    pl.semaphore_signal(barrier, inc=1, device_id=sibling, device_id_type=pl.DeviceIdType.MESH)

    for j in range(2):
        fresh_loads[0][j].start()
    for i in (3, 5, 2, 6, 1, 7, 0):
        weight_load(i).start()
    for j in range(2):
        fresh_loads[1][j].start()
    for load in loads[1:]:
        load.start()

    def ring_copy(direction, slot, tile):
        spot = pl.ds(tile * TILE, TILE)
        return pltpu.make_async_remote_copy(
            src_ref=outgoing.at[direction, slot, spot],
            dst_ref=incoming.at[direction, slot, spot],
            send_sem=ring_send.at[direction, slot, tile],
            recv_sem=ring_recv.at[direction, slot, tile],
            device_id={"tensor": (z + 1 - 2 * direction + Z) % Z},
            device_id_type=pl.DeviceIdType.MESH,
        )

    ways = [(direction, tile) for tile in range(tiles) for direction in range(2)]

    def lines(direction, is_long, tile):
        side = direction if is_long else 1 - direction
        return pl.ds(side * half + tile * TILE, TILE)

    def ring_step(slot, send):
        is_long, step, before = SLOTS[slot]
        if is_long and step == 0:
            weight_load(4).wait()
        elif not is_long:
            weight_load(4 - step).wait()
            weight_load(4 + step).wait()
        for direction, tile in ways:
            spot = pl.ds(tile * TILE, TILE)
            term = dot(acts[lines(direction, is_long, tile)], weight[4 - step + 2 * step * direction])
            if before is not None:
                ring_copy(direction, before, tile).wait_recv()
                term = term + incoming[direction, before, spot].astype(F32)
            outgoing[direction, slot, spot] = term.astype(BF16)
            if send:
                ring_copy(direction, slot, tile).start()

    def line_of(j, second, of_core):
        return ((j * 2 + of_core) * SIDE + second) * SIDE

    def across_line(first):
        return (first % 2) * 2 + first // 2

    def gather_copy(g, j, kind, direction=0, incoming_side=False):
        held = gathers[g][0]
        first, second = (x, y) if j == 0 else (y, x)
        first_axis, second_axis = (0, 1) if j == 0 else (1, 0)
        sign = 1 - 2 * direction
        back = -sign if incoming_side else 0
        here = across_line(first)
        pair = (1 - first % 2) * 2
        far = across_line((first + 2) % SIDE)
        part = pl.ds(direction * (rank // 2), rank // 2)

        def line(step):
            return line_of(j, (second + step + SIDE) % SIDE, core)

        axis = second_axis
        if kind == FIRST:
            axis = first_axis
            ref = held.at[line(0) + across_line((first + back + SIDE) % SIDE)]
        elif kind == FIRST_FAR:
            axis = first_axis
            ref = held.at[line(0) + across_line((first + back - sign + SIDE) % SIDE), part]
        elif kind == SECOND:
            ref = held.at[line(back) + here]
        elif kind == SECOND_PAIR:
            ref = held.at[pl.ds(line(back) + pair, 2)]
        elif kind == SECOND_FAR:
            ref = held.at[line(back) + far]
        elif kind == OWN_ON:
            ref = held.at[line(back - sign) + here, part]
        elif kind == PAIR_ON:
            ref = held.at[line(back - sign) + pair + direction]
        else:
            ref = held.at[line(back - sign) + far, part]
        number = 2 * kind + direction
        return pltpu.make_async_remote_copy(
            src_ref=ref, dst_ref=ref,
            send_sem=gather_send.at[g, j, number], recv_sem=gather_recv.at[g, j, number],
            device_id=along(axis, sign), device_id_type=pl.DeviceIdType.MESH,
        )

    def across_copy(g, j, number, incoming_side=False):
        held = gathers[g][0]
        second = y if j == 0 else x
        moved = (second + (0, -1, 1, 2)[number] + SIDE) % SIDE
        ref = held.at[pl.ds(line_of(j, moved, 1 - core if incoming_side else core), SIDE)]
        return pltpu.make_async_remote_copy(
            src_ref=ref, dst_ref=ref,
            send_sem=gather_send.at[g, j, ROWS_ACROSS + number], recv_sem=gather_recv.at[g, j, ROWS_ACROSS + number],
            device_id=sibling, device_id_type=pl.DeviceIdType.MESH,
        )

    both = [(j, direction) for j in range(2) for direction in range(2)]

    def send_all(g, *kinds):
        for kind in kinds:
            for j, direction in both:
                gather_copy(g, j, kind, direction).start()

    def take_all(g, *kinds):
        for kind in kinds:
            for j, direction in both:
                gather_copy(g, j, kind, direction, True).wait_recv()

    def send_across(g, *numbers):
        for number in numbers:
            for j in range(2):
                across_copy(g, j, number).start()

    def gather_0(g):
        for j in range(2):
            fresh_loads[g][j].wait()
        send_all(g, FIRST, SECOND)

    def gather_1(g):
        take_all(g, FIRST)
        send_all(g, FIRST_FAR, SECOND_PAIR)

    def gather_2(g):
        take_all(g, FIRST_FAR)
        send_all(g, SECOND_FAR)
        send_across(g, 0)

    def gather_3(g):
        take_all(g, SECOND)
        send_all(g, OWN_ON)
        take_all(g, SECOND_PAIR)
        send_all(g, PAIR_ON)

    def gather_4(g):
        take_all(g, SECOND_FAR)
        send_all(g, FAR_ON)
        send_across(g, 1, 2)

    def gather_5(g):
        take_all(g, OWN_ON, PAIR_ON, FAR_ON)
        send_across(g, 3)

    def gather_6(g):
        for number in range(4):
            for j in range(2):
                across_copy(g, j, number, True).wait_recv()

    def match(b):
        def body(i, carry):
            found, where = carry
            hit = renewed[i] == ids[b]
            return jnp.where(hit, 1, found), jnp.where(hit, i, where)

        return lax.fori_loop(0, renewed_hbm.shape[0], body, (jnp.int32(0), jnp.int32(0)))

    def chosen(held, cached, b, found, where):
        j, of_core, px, py = where % 2, (where // 2) % 2, (where // 4) % SIDE, where // 16
        second, first = jnp.where(j == 0, py, px), jnp.where(j == 0, px, py)
        return jnp.where(found > 0, held[line_of(j, second, of_core) + across_line(first)], cached[b])

    piece = rows // Z

    def part_copy(i):
        return pltpu.make_async_remote_copy(
            src_ref=part_out.at[(z + i) % Z], dst_ref=part_in.at[i],
            send_sem=part_send.at[i], recv_sem=part_recv.at[i],
            device_id={"tensor": (z + i) % Z}, device_id_type=pl.DeviceIdType.MESH,
        )

    def shrunk_copy(i):
        return pltpu.make_async_remote_copy(
            src_ref=shrunk.at[0], dst_ref=shrunk.at[i],
            send_sem=shrunk_send.at[i], recv_sem=shrunk_recv.at[i],
            device_id={"tensor": (z + i) % Z}, device_id_type=pl.DeviceIdType.MESH,
        )

    def shrink_parts(matches):
        for b in range(blocks):
            factor = chosen(every_a, cached_a, b, *matches[b])
            part = lax.dot_general(
                acts[pl.ds(b * TILE, TILE)], factor, (((1,), (1,)), ((), ())), preferred_element_type=F32
            )
            for q in range(TILE // piece):
                upper = part[q * piece : q * piece + piece // 2]
                lower = part[q * piece + piece // 2 : (q + 1) * piece]
                part_out[b * (TILE // piece) + q] = jnp.concatenate([upper, lower], axis=1).astype(BF16)
        for i in range(1, Z):
            part_copy(i).start()

    def shrink_sum():
        value = part_out[z].astype(F32)
        for i in range(1, Z):
            part_copy(i).wait_recv()
            value = value + part_in[i].astype(F32)
        shrunk[0] = value.astype(BF16)
        for i in range(1, Z):
            shrunk_copy(i).start()

    def expand(matches):
        for i in range(1, Z):
            shrunk_copy(i).wait_recv()
        for b in range(blocks):
            factor = chosen(every_b, cached_b, b, *matches[b])
            lines = []
            for q in range(TILE // piece):
                packed = shrunk[(z + Z - b * (TILE // piece) - q) % Z].astype(F32)
                lines += [packed[:, :rank], packed[:, rank:]]
            lines = jnp.concatenate(lines, axis=0).astype(BF16)
            spot = pl.ds(b * TILE, TILE)
            total[spot] = total[spot] + adapter_scale * dot(lines, factor)

    def own_base():
        weight_load(0).wait()
        for i in range(rows // TILE):
            spot = pl.ds(i * TILE, TILE)
            total[spot] = dot(acts[spot], weight[0])

    def add_short():
        for direction, tile in ways:
            ring_copy(direction, LAST_SHORT, tile).wait_recv()
            spot = lines(direction, False, tile)
            total[spot] = total[spot] + incoming[direction, LAST_SHORT, pl.ds(tile * TILE, TILE)].astype(F32)

    def out_copy(direction, tile):
        spot = lines(direction, True, tile)
        return pltpu.make_async_copy(result.at[spot], out_hbm.at[spot], out_sem.at[direction, tile])

    def finish():
        for direction, tile in ways:
            ring_copy(direction, LAST_LONG, tile).wait_recv()
            spot = lines(direction, True, tile)
            got = incoming[direction, LAST_LONG, pl.ds(tile * TILE, TILE)]
            result[spot] = (total[spot] + got.astype(F32)).astype(BF16)
            out_copy(direction, tile).start()

    loads[0].wait()
    ring_step(0, False)
    pl.semaphore_wait(barrier, Z - 1 + 5)

    for direction, tile in ways:
        ring_copy(direction, 0, tile).start()
    gather_0(0)
    ring_step(1, True)
    own_base()
    for load in loads[1:]:
        load.wait()
    matches = [match(b) for b in range(blocks)]
    gather_1(0)
    ring_step(2, True)
    gather_2(0)
    gather_0(1)
    ring_step(3, True)
    gather_3(0)
    gather_1(1)
    ring_step(4, True)
    gather_4(0)
    gather_2(1)
    gather_5(0)
    ring_step(5, True)
    gather_6(0)
    shrink_parts(matches)
    gather_3(1)
    ring_step(6, True)
    shrink_sum()
    gather_4(1)
    gather_5(1)
    add_short()
    gather_6(1)
    expand(matches)
    finish()

    for slot in range(len(SLOTS)):
        for direction, tile in ways:
            ring_copy(direction, slot, tile).wait_send()
    for g in range(2):
        for kind in range(8):
            for j, direction in both:
                gather_copy(g, j, kind, direction).wait_send()
        for number in range(4):
            for j in range(2):
                across_copy(g, j, number).wait_send()
    for i in range(1, Z):
        part_copy(i).wait_send()
        shrunk_copy(i).wait_send()
    for direction, tile in ways:
        out_copy(direction, tile).wait()


def shards(acts, weight, block_ids, cached_a, cached_b, renewed_module_numbers, fresh_a, renewed_second_matrices):
    rows, depth = acts.shape
    width = cached_b.shape[2]
    blocks, rank = cached_b.shape[0], cached_b.shape[1]
    tiles = rows // 2 // TILE
    slots = len(SLOTS)
    dma = pltpu.SemaphoreType.DMA
    return pl.pallas_call(
        kernel,
        out_shape=jax.ShapeDtypeStruct((rows, width), BF16),
        in_specs=[pl.BlockSpec(memory_space=pl.ANY)] * 8,
        out_specs=pl.BlockSpec(memory_space=pl.ANY),
        scratch_shapes=[
            pltpu.VMEM((rows, depth), BF16),
            pltpu.VMEM((Z, depth, width), BF16),
            pltpu.SMEM(block_ids.shape, jnp.int32),
            pltpu.SMEM(renewed_module_numbers.shape, jnp.int32),
            pltpu.VMEM((blocks, rank, depth), BF16),
            pltpu.VMEM((blocks, rank, width), BF16),
            pltpu.VMEM((2 * 2 * SIDE * SIDE, rank, depth), BF16),
            pltpu.VMEM((2 * 2 * SIDE * SIDE, rank, width), BF16),
            pltpu.VMEM((2, slots, rows // 2, width), BF16),
            pltpu.VMEM((2, slots, rows // 2, width), BF16),
            pltpu.VMEM((rows, width), F32),
            pltpu.VMEM((rows, width), BF16),
            pltpu.VMEM((Z, rows // Z // 2, 2 * rank), BF16),
            pltpu.VMEM((Z, rows // Z // 2, 2 * rank), BF16),
            pltpu.VMEM((Z, rows // Z // 2, 2 * rank), BF16),
            dma((5,)),
            dma((Z,)),
            dma((2, 2)),
            dma((2, tiles)),
            dma((2, slots, tiles)),
            dma((2, slots, tiles)),
            dma((2, 2, 20)),
            dma((2, 2, 20)),
            dma((Z,)),
            dma((Z,)),
            dma((Z,)),
            dma((Z,)),
        ],
        compiler_params=pltpu.CompilerParams(
            collective_id=0, has_side_effects=True, vmem_limit_bytes=60 * 1024 * 1024
        ),
    )(
        acts, weight, block_ids, jnp.swapaxes(cached_a, 1, 2), cached_b,
        renewed_module_numbers, jnp.swapaxes(fresh_a, 1, 2), renewed_second_matrices,
    )


def solution(mesh):
    return jax.shard_map(
        shards,
        mesh=mesh,
        in_specs=(
            P("dp", "tensor"),
            P("tensor", None),
            P("dp"),
            P("dp", "tensor", None),
            P("dp", None, "tensor"),
            P(),
            P("dp", "tensor", None),
            P("dp", None, "tensor"),
        ),
        out_specs=P("dp", "tensor"),
        check_vma=False,
    )
```

```python
import jax
import jax.numpy as jnp
from jax import lax
from jax.experimental import pallas as pl
from jax.experimental.pallas import tpu as pltpu
from jax.sharding import PartitionSpec as P

adapter_scale = 2.0
Z = 8
SIDE = 4
TILE = 128
BF16 = jnp.bfloat16
F32 = jnp.float32

SLOTS = (
    (True, 0, None),
    (False, 1, None),
    (True, 1, 0),
    (False, 2, 1),
    (True, 2, 2),
    (False, 3, 3),
    (True, 3, 4),
)
LAST_LONG, LAST_SHORT = 6, 5

FIRST, SECOND, FIRST_FAR, SECOND_PAIR, SECOND_FAR, OWN_ON, PAIR_ON, FAR_ON = range(8)
ROWS_ACROSS = 16


def dot(a, b):
    return jnp.dot(a, b, preferred_element_type=F32)


def kernel(
    acts_hbm, weight_hbm, ids_hbm, cached_a_hbm, cached_b_hbm, renewed_hbm, fresh_a_hbm, fresh_b_hbm,
    result,
    acts, weight, ids, renewed, cached_a, cached_b, every_a, every_b,
    outgoing, incoming, total, part_out, part_in, shrunk,
    load_sem, weight_sem, fresh_sem,
    ring_send, ring_recv, gather_send, gather_recv, part_send, part_recv, shrunk_send, shrunk_recv,
):
    z = lax.axis_index("tensor")
    dp = lax.axis_index("dp")
    core = dp % 2
    x = (dp // 2) % SIDE
    y = dp // (2 * SIDE)
    depth, width = weight.shape[1], weight.shape[2]
    blocks = ids_hbm.shape[0]
    rows = acts.shape[0]
    half = rows // 2
    tiles = half // TILE
    rank = cached_a.shape[1]

    def at_xy(px, py, pc):
        return {"dp": (py * SIDE + px) * 2 + pc}

    def along(axis, step):
        if axis == 0:
            return at_xy((x + step + SIDE) % SIDE, y, core)
        return at_xy(x, (y + step + SIDE) % SIDE, core)

    sibling = at_xy(x, y, 1 - core)

    def weight_load(i):
        column = pl.multiple_of((z + i) % Z * width, 128)
        return pltpu.make_async_copy(weight_hbm.at[:, pl.ds(column, width)], weight.at[i], weight_sem.at[i])

    loads = [
        pltpu.make_async_copy(acts_hbm, acts, load_sem.at[0]),
        pltpu.make_async_copy(cached_a_hbm, cached_a, load_sem.at[1]),
        pltpu.make_async_copy(cached_b_hbm, cached_b, load_sem.at[2]),
        pltpu.make_async_copy(ids_hbm, ids, load_sem.at[3]),
        pltpu.make_async_copy(renewed_hbm, renewed, load_sem.at[4]),
    ]
    mine = (
        (core * SIDE + y) * SIDE + (x % 2) * 2 + x // 2,
        ((2 + core) * SIDE + x) * SIDE + (y % 2) * 2 + y // 2,
    )
    gathers = ((every_a, fresh_a_hbm), (every_b, fresh_b_hbm))
    fresh_loads = [
        [pltpu.make_async_copy(source.at[j], held.at[mine[j]], fresh_sem.at[g, j]) for j in range(2)]
        for g, (held, source) in enumerate(gathers)
    ]

    loads[0].start()
    weight_load(4).start()

    barrier = pltpu.get_barrier_semaphore()
    for i in range(1, Z):
        pl.semaphore_signal(barrier, inc=1, device_id={"tensor": (z + i) % Z}, device_id_type=pl.DeviceIdType.MESH)
    for axis in range(2):
        for step in (1, -1):
            pl.semaphore_signal(barrier, inc=1, device_id=along(axis, step), device_id_type=pl.DeviceIdType.MESH)
    pl.semaphore_signal(barrier, inc=1, device_id=sibling, device_id_type=pl.DeviceIdType.MESH)

    for j in range(2):
        fresh_loads[0][j].start()
    for i in (3, 5, 2, 6, 1, 7, 0):
        weight_load(i).start()
    for j in range(2):
        fresh_loads[1][j].start()
    for load in loads[1:]:
        load.start()

    def ring_copy(direction, slot, tile):
        spot = pl.ds(tile * TILE, TILE)
        return pltpu.make_async_remote_copy(
            src_ref=outgoing.at[direction, slot, spot],
            dst_ref=incoming.at[direction, slot, spot],
            send_sem=ring_send.at[direction, slot, tile],
            recv_sem=ring_recv.at[direction, slot, tile],
            device_id={"tensor": (z + 1 - 2 * direction + Z) % Z},
            device_id_type=pl.DeviceIdType.MESH,
        )

    ways = [(direction, tile) for tile in range(tiles) for direction in range(2)]

    def lines(direction, is_long, tile):
        side = direction if is_long else 1 - direction
        return pl.ds(side * half + tile * TILE, TILE)

    def ring_step(slot, send):
        is_long, step, before = SLOTS[slot]
        if is_long and step == 0:
            weight_load(4).wait()
        elif not is_long:
            weight_load(4 - step).wait()
            weight_load(4 + step).wait()
        for direction, tile in ways:
            spot = pl.ds(tile * TILE, TILE)
            term = dot(acts[lines(direction, is_long, tile)], weight[4 - step + 2 * step * direction])
            if before is not None:
                ring_copy(direction, before, tile).wait_recv()
                term = term + incoming[direction, before, spot].astype(F32)
            outgoing[direction, slot, spot] = term.astype(BF16)
            if send:
                ring_copy(direction, slot, tile).start()

    def line_of(j, second, of_core):
        return ((j * 2 + of_core) * SIDE + second) * SIDE

    def across_line(first):
        return (first % 2) * 2 + first // 2

    def gather_copy(g, j, kind, direction=0, incoming_side=False):
        held = gathers[g][0]
        first, second = (x, y) if j == 0 else (y, x)
        first_axis, second_axis = (0, 1) if j == 0 else (1, 0)
        sign = 1 - 2 * direction
        back = -sign if incoming_side else 0
        here = across_line(first)
        pair = (1 - first % 2) * 2
        far = across_line((first + 2) % SIDE)
        part = pl.ds(direction * (rank // 2), rank // 2)

        def line(step):
            return line_of(j, (second + step + SIDE) % SIDE, core)

        axis = second_axis
        if kind == FIRST:
            axis = first_axis
            ref = held.at[line(0) + across_line((first + back + SIDE) % SIDE)]
        elif kind == FIRST_FAR:
            axis = first_axis
            ref = held.at[line(0) + across_line((first + back - sign + SIDE) % SIDE), part]
        elif kind == SECOND:
            ref = held.at[line(back) + here]
        elif kind == SECOND_PAIR:
            ref = held.at[pl.ds(line(back) + pair, 2)]
        elif kind == SECOND_FAR:
            ref = held.at[line(back) + far]
        elif kind == OWN_ON:
            ref = held.at[line(back - sign) + here, part]
        elif kind == PAIR_ON:
            ref = held.at[line(back - sign) + pair + direction]
        else:
            ref = held.at[line(back - sign) + far, part]
        number = 2 * kind + direction
        return pltpu.make_async_remote_copy(
            src_ref=ref, dst_ref=ref,
            send_sem=gather_send.at[g, j, number], recv_sem=gather_recv.at[g, j, number],
            device_id=along(axis, sign), device_id_type=pl.DeviceIdType.MESH,
        )

    def across_copy(g, j, number, incoming_side=False):
        held = gathers[g][0]
        second = y if j == 0 else x
        moved = (second + (0, -1, 1, 2)[number] + SIDE) % SIDE
        ref = held.at[pl.ds(line_of(j, moved, 1 - core if incoming_side else core), SIDE)]
        return pltpu.make_async_remote_copy(
            src_ref=ref, dst_ref=ref,
            send_sem=gather_send.at[g, j, ROWS_ACROSS + number], recv_sem=gather_recv.at[g, j, ROWS_ACROSS + number],
            device_id=sibling, device_id_type=pl.DeviceIdType.MESH,
        )

    both = [(j, direction) for j in range(2) for direction in range(2)]

    def send_all(g, *kinds):
        for kind in kinds:
            for j, direction in both:
                gather_copy(g, j, kind, direction).start()

    def take_all(g, *kinds):
        for kind in kinds:
            for j, direction in both:
                gather_copy(g, j, kind, direction, True).wait_recv()

    def send_across(g, *numbers):
        for number in numbers:
            for j in range(2):
                across_copy(g, j, number).start()

    def gather_0(g):
        for j in range(2):
            fresh_loads[g][j].wait()
        send_all(g, FIRST, SECOND)

    def gather_1(g):
        take_all(g, FIRST)
        send_all(g, FIRST_FAR, SECOND_PAIR)

    def gather_2(g):
        take_all(g, FIRST_FAR)
        send_all(g, SECOND_FAR)
        take_all(g, SECOND)
        send_all(g, OWN_ON)
        send_across(g, 0)

    def gather_3(g):
        take_all(g, SECOND_PAIR)
        send_all(g, PAIR_ON)

    def gather_4(g):
        take_all(g, SECOND_FAR)
        send_all(g, FAR_ON)
        send_across(g, 1, 2)

    def gather_5(g):
        take_all(g, OWN_ON, PAIR_ON, FAR_ON)
        send_across(g, 3)

    def gather_6(g):
        for number in range(4):
            for j in range(2):
                across_copy(g, j, number, True).wait_recv()

    def match(b):
        def body(i, carry):
            found, where = carry
            hit = renewed[i] == ids[b]
            return jnp.where(hit, 1, found), jnp.where(hit, i, where)

        return lax.fori_loop(0, renewed_hbm.shape[0], body, (jnp.int32(0), jnp.int32(0)))

    def chosen(held, cached, b, found, where):
        j, of_core, px, py = where % 2, (where // 2) % 2, (where // 4) % SIDE, where // 16
        second, first = jnp.where(j == 0, py, px), jnp.where(j == 0, px, py)
        return jnp.where(found > 0, held[line_of(j, second, of_core) + across_line(first)], cached[b])

    piece = rows // Z

    def part_copy(i):
        return pltpu.make_async_remote_copy(
            src_ref=part_out.at[(z + i) % Z], dst_ref=part_in.at[i],
            send_sem=part_send.at[i], recv_sem=part_recv.at[i],
            device_id={"tensor": (z + i) % Z}, device_id_type=pl.DeviceIdType.MESH,
        )

    def shrunk_copy(i):
        return pltpu.make_async_remote_copy(
            src_ref=shrunk.at[0], dst_ref=shrunk.at[i],
            send_sem=shrunk_send.at[i], recv_sem=shrunk_recv.at[i],
            device_id={"tensor": (z + i) % Z}, device_id_type=pl.DeviceIdType.MESH,
        )

    def shrink_parts(matches):
        for b in range(blocks):
            factor = chosen(every_a, cached_a, b, *matches[b])
            part = lax.dot_general(
                acts[pl.ds(b * TILE, TILE)], factor, (((1,), (1,)), ((), ())), preferred_element_type=F32
            )
            for q in range(TILE // piece):
                upper = part[q * piece : q * piece + piece // 2]
                lower = part[q * piece + piece // 2 : (q + 1) * piece]
                part_out[b * (TILE // piece) + q] = jnp.concatenate([upper, lower], axis=1).astype(BF16)
        for i in range(1, Z):
            part_copy(i).start()

    def shrink_sum():
        value = part_out[z].astype(F32)
        for i in range(1, Z):
            part_copy(i).wait_recv()
            value = value + part_in[i].astype(F32)
        shrunk[0] = value.astype(BF16)
        for i in range(1, Z):
            shrunk_copy(i).start()

    def expand(matches):
        for i in range(1, Z):
            shrunk_copy(i).wait_recv()
        for b in range(blocks):
            factor = chosen(every_b, cached_b, b, *matches[b])
            lines = []
            for q in range(TILE // piece):
                packed = shrunk[(z + Z - b * (TILE // piece) - q) % Z].astype(F32)
                lines += [packed[:, :rank], packed[:, rank:]]
            lines = jnp.concatenate(lines, axis=0).astype(BF16)
            spot = pl.ds(b * TILE, TILE)
            total[spot] = total[spot] + adapter_scale * dot(lines, factor)

    def own_base():
        weight_load(0).wait()
        for i in range(rows // TILE):
            spot = pl.ds(i * TILE, TILE)
            total[spot] = dot(acts[spot], weight[0])

    def add_short():
        for direction, tile in ways:
            ring_copy(direction, LAST_SHORT, tile).wait_recv()
            spot = lines(direction, False, tile)
            total[spot] = total[spot] + incoming[direction, LAST_SHORT, pl.ds(tile * TILE, TILE)].astype(F32)

    def finish():
        for direction, tile in ways:
            ring_copy(direction, LAST_LONG, tile).wait_recv()
            spot = lines(direction, True, tile)
            got = incoming[direction, LAST_LONG, pl.ds(tile * TILE, TILE)]
            result[spot] = (total[spot] + got.astype(F32)).astype(BF16)

    loads[0].wait()
    ring_step(0, False)
    pl.semaphore_wait(barrier, Z - 1 + 5)

    for direction, tile in ways:
        ring_copy(direction, 0, tile).start()
    gather_0(0)
    ring_step(1, True)
    own_base()
    for load in loads[1:]:
        load.wait()
    matches = [match(b) for b in range(blocks)]
    gather_1(0)
    ring_step(2, True)
    gather_2(0)
    gather_3(0)
    ring_step(3, True)
    gather_4(0)
    gather_0(1)
    ring_step(4, True)
    gather_5(0)
    gather_1(1)
    gather_6(0)
    shrink_parts(matches)
    gather_2(1)
    ring_step(5, True)
    gather_3(1)
    gather_4(1)
    shrink_sum()
    ring_step(6, True)
    gather_5(1)
    gather_6(1)
    add_short()
    expand(matches)
    finish()

    for slot in range(len(SLOTS)):
        for direction, tile in ways:
            ring_copy(direction, slot, tile).wait_send()
    for g in range(2):
        for kind in range(8):
            for j, direction in both:
                gather_copy(g, j, kind, direction).wait_send()
        for number in range(4):
            for j in range(2):
                across_copy(g, j, number).wait_send()
    for i in range(1, Z):
        part_copy(i).wait_send()
        shrunk_copy(i).wait_send()


def shards(acts, weight, block_ids, cached_a, cached_b, renewed_module_numbers, fresh_a, renewed_second_matrices):
    rows, depth = acts.shape
    width = cached_b.shape[2]
    blocks, rank = cached_b.shape[0], cached_b.shape[1]
    tiles = rows // 2 // TILE
    slots = len(SLOTS)
    dma = pltpu.SemaphoreType.DMA
    return pl.pallas_call(
        kernel,
        out_shape=pltpu.VMEM((rows, width), BF16),
        in_specs=[pl.BlockSpec(memory_space=pl.ANY)] * 8,
        out_specs=pl.BlockSpec(memory_space=pltpu.VMEM),
        scratch_shapes=[
            pltpu.VMEM((rows, depth), BF16),
            pltpu.VMEM((Z, depth, width), BF16),
            pltpu.SMEM(block_ids.shape, jnp.int32),
            pltpu.SMEM(renewed_module_numbers.shape, jnp.int32),
            pltpu.VMEM((blocks, rank, depth), BF16),
            pltpu.VMEM((blocks, rank, width), BF16),
            pltpu.VMEM((2 * 2 * SIDE * SIDE, rank, depth), BF16),
            pltpu.VMEM((2 * 2 * SIDE * SIDE, rank, width), BF16),
            pltpu.VMEM((2, slots, rows // 2, width), BF16),
            pltpu.VMEM((2, slots, rows // 2, width), BF16),
            pltpu.VMEM((rows, width), F32),
            pltpu.VMEM((Z, rows // Z // 2, 2 * rank), BF16),
            pltpu.VMEM((Z, rows // Z // 2, 2 * rank), BF16),
            pltpu.VMEM((Z, rows // Z // 2, 2 * rank), BF16),
            dma((5,)),
            dma((Z,)),
            dma((2, 2)),
            dma((2, slots, tiles)),
            dma((2, slots, tiles)),
            dma((2, 2, 20)),
            dma((2, 2, 20)),
            dma((Z,)),
            dma((Z,)),
            dma((Z,)),
            dma((Z,)),
        ],
        compiler_params=pltpu.CompilerParams(
            collective_id=0, has_side_effects=True, vmem_limit_bytes=60 * 1024 * 1024
        ),
    )(
        acts, weight, block_ids, jnp.swapaxes(cached_a, 1, 2), cached_b,
        renewed_module_numbers, jnp.swapaxes(fresh_a, 1, 2), renewed_second_matrices,
    )


def solution(mesh):
    return jax.shard_map(
        shards,
        mesh=mesh,
        in_specs=(
            P("dp", "tensor"),
            P("tensor", None),
            P("dp"),
            P("dp", "tensor", None),
            P("dp", None, "tensor"),
            P(),
            P("dp", "tensor", None),
            P("dp", None, "tensor"),
        ),
        out_specs=P("dp", "tensor"),
        check_vma=False,
    )
```

```python
import jax
import jax.numpy as jnp
from jax import lax
from jax.experimental import pallas as pl
from jax.experimental.pallas import tpu as pltpu
from jax.sharding import PartitionSpec as P

adapter_scale = 2.0
Z = 8
SIDE = 4
TILE = 128
PARTS = 2
BF16 = jnp.bfloat16
F32 = jnp.float32

SLOTS = (
    (True, 0, None),
    (False, 1, None),
    (True, 1, 0),
    (False, 2, 1),
    (True, 2, 2),
    (False, 3, 3),
    (True, 3, 4),
)
LAST_LONG, LAST_SHORT = 6, 5

FIRST, SECOND, FIRST_FAR, SECOND_PAIR, SECOND_FAR, OWN_ON, PAIR_ON, FAR_ON = range(8)
ROWS_ACROSS = 16


def dot(a, b):
    return jnp.dot(a, b, preferred_element_type=F32)


def kernel(
    acts_hbm, weight_hbm, ids_hbm, cached_a_hbm, cached_b_hbm, renewed_hbm, fresh_a_hbm, fresh_b_hbm,
    result,
    acts, weight, ids, renewed, cached_a, cached_b, every_a, every_b,
    outgoing, incoming, total, part_out, part_in, merged, shrunk,
    load_sem, weight_sem, fresh_sem,
    ring_send, ring_recv, gather_send, gather_recv, part_send, part_recv, shrunk_send, shrunk_recv,
):
    z = lax.axis_index("tensor")
    dp = lax.axis_index("dp")
    core = dp % 2
    x = (dp // 2) % SIDE
    y = dp // (2 * SIDE)
    depth, width = weight.shape[1], weight.shape[2]
    blocks = ids_hbm.shape[0]
    rows = acts.shape[0]
    half = rows // 2
    tiles = half // TILE
    rank = cached_a.shape[1]

    def at_xy(px, py, pc):
        return {"dp": (py * SIDE + px) * 2 + pc}

    def along(axis, step):
        if axis == 0:
            return at_xy((x + step + SIDE) % SIDE, y, core)
        return at_xy(x, (y + step + SIDE) % SIDE, core)

    sibling = at_xy(x, y, 1 - core)

    def weight_load(i):
        column = pl.multiple_of((z + i) % Z * width, 128)
        return pltpu.make_async_copy(weight_hbm.at[:, pl.ds(column, width)], weight.at[i], weight_sem.at[i])

    loads = [
        pltpu.make_async_copy(acts_hbm, acts, load_sem.at[0]),
        pltpu.make_async_copy(cached_a_hbm, cached_a, load_sem.at[1]),
        pltpu.make_async_copy(cached_b_hbm, cached_b, load_sem.at[2]),
        pltpu.make_async_copy(ids_hbm, ids, load_sem.at[3]),
        pltpu.make_async_copy(renewed_hbm, renewed, load_sem.at[4]),
    ]
    mine = (
        (core * SIDE + y) * SIDE + (x % 2) * 2 + x // 2,
        ((2 + core) * SIDE + x) * SIDE + (y % 2) * 2 + y // 2,
    )
    gathers = ((every_a, fresh_a_hbm), (every_b, fresh_b_hbm))
    fresh_loads = [
        [pltpu.make_async_copy(source.at[j], held.at[mine[j]], fresh_sem.at[g, j]) for j in range(2)]
        for g, (held, source) in enumerate(gathers)
    ]

    barrier = pltpu.get_barrier_semaphore()
    for i in (1, Z - 1, 2, Z - 2, 3, Z - 3, 4):
        pl.semaphore_signal(barrier, inc=1, device_id={"tensor": (z + i) % Z}, device_id_type=pl.DeviceIdType.MESH)
    for axis in range(2):
        for step in (1, -1):
            pl.semaphore_signal(barrier, inc=1, device_id=along(axis, step), device_id_type=pl.DeviceIdType.MESH)
    pl.semaphore_signal(barrier, inc=1, device_id=sibling, device_id_type=pl.DeviceIdType.MESH)

    weight_load(4).start()
    loads[0].start()
    for j in range(2):
        fresh_loads[0][j].start()

    def ring_copy(direction, slot, tile, part=0, parts=1):
        spot = pl.ds(tile * TILE + part * (TILE // parts), TILE // parts)
        return pltpu.make_async_remote_copy(
            src_ref=outgoing.at[direction, slot, spot],
            dst_ref=incoming.at[direction, slot, spot],
            send_sem=ring_send.at[direction, slot, tile * PARTS + part],
            recv_sem=ring_recv.at[direction, slot, tile * PARTS + part],
            device_id={"tensor": (z + 1 - 2 * direction + Z) % Z},
            device_id_type=pl.DeviceIdType.MESH,
        )

    ways = [(direction, tile) for tile in range(tiles) for direction in range(2)]

    def lines(direction, is_long, tile):
        side = direction if is_long else 1 - direction
        return pl.ds(side * half + tile * TILE, TILE)

    def ring_piece(slot, direction, tile):
        is_long, step, before = SLOTS[slot]
        spot = pl.ds(tile * TILE, TILE)
        term = dot(acts[lines(direction, is_long, tile)], weight[4 - step + 2 * step * direction])
        if before is not None:
            ring_copy(direction, before, tile).wait_recv()
            term = term + incoming[direction, before, spot].astype(F32)
        outgoing[direction, slot, spot] = term.astype(BF16)

    def ring_send_piece(slot, direction, tile):
        parts = PARTS if slot == LAST_LONG else 1
        for part in range(parts):
            ring_copy(direction, slot, tile, part, parts).start()

    def ring_step(slot):
        is_long, step, _ = SLOTS[slot]
        if not is_long:
            weight_load(4 - step).wait()
            weight_load(4 + step).wait()
        for tile in range(tiles):
            ring_tile(slot, tile)

    def ring_tile(slot, tile, send=True):
        for direction in range(2):
            ring_piece(slot, direction, tile)
            if send:
                ring_send_piece(slot, direction, tile)

    def ring_out(slot, tile):
        for direction in range(2):
            ring_send_piece(slot, direction, tile)

    def line_of(j, second, of_core):
        return ((j * 2 + of_core) * SIDE + second) * SIDE

    def across_line(first):
        return (first % 2) * 2 + first // 2

    def gather_copy(g, j, kind, direction=0, incoming_side=False):
        held = gathers[g][0]
        first, second = (x, y) if j == 0 else (y, x)
        first_axis, second_axis = (0, 1) if j == 0 else (1, 0)
        sign = 1 - 2 * direction
        back = -sign if incoming_side else 0
        here = across_line(first)
        pair = (1 - first % 2) * 2
        far = across_line((first + 2) % SIDE)
        part = pl.ds(direction * (rank // 2), rank // 2)

        def line(step):
            return line_of(j, (second + step + SIDE) % SIDE, core)

        axis = second_axis
        if kind == FIRST:
            axis = first_axis
            ref = held.at[line(0) + across_line((first + back + SIDE) % SIDE)]
        elif kind == FIRST_FAR:
            axis = first_axis
            ref = held.at[line(0) + across_line((first + back - sign + SIDE) % SIDE), part]
        elif kind == SECOND:
            ref = held.at[line(back) + here]
        elif kind == SECOND_PAIR:
            ref = held.at[pl.ds(line(back) + pair, 2)]
        elif kind == SECOND_FAR:
            ref = held.at[line(back) + far]
        elif kind == OWN_ON:
            ref = held.at[line(back - sign) + here, part]
        elif kind == PAIR_ON:
            ref = held.at[line(back - sign) + pair + direction]
        else:
            ref = held.at[line(back - sign) + far, part]
        number = 2 * kind + direction
        return pltpu.make_async_remote_copy(
            src_ref=ref, dst_ref=ref,
            send_sem=gather_send.at[g, j, number], recv_sem=gather_recv.at[g, j, number],
            device_id=along(axis, sign), device_id_type=pl.DeviceIdType.MESH,
        )

    def across_copy(g, j, number, incoming_side=False):
        held = gathers[g][0]
        second = y if j == 0 else x
        moved = (second + (0, -1, 1, 2)[number] + SIDE) % SIDE
        ref = held.at[pl.ds(line_of(j, moved, 1 - core if incoming_side else core), SIDE)]
        return pltpu.make_async_remote_copy(
            src_ref=ref, dst_ref=ref,
            send_sem=gather_send.at[g, j, ROWS_ACROSS + number], recv_sem=gather_recv.at[g, j, ROWS_ACROSS + number],
            device_id=sibling, device_id_type=pl.DeviceIdType.MESH,
        )

    both = [(j, direction) for j in range(2) for direction in range(2)]

    def send_all(g, *kinds):
        for kind in kinds:
            for j, direction in both:
                gather_copy(g, j, kind, direction).start()

    def take_all(g, *kinds):
        for kind in kinds:
            for j, direction in both:
                gather_copy(g, j, kind, direction, True).wait_recv()

    def send_across(g, *numbers):
        for number in numbers:
            for j in range(2):
                across_copy(g, j, number).start()

    def gather_0(g):
        for j in range(2):
            fresh_loads[g][j].wait()
        send_all(g, FIRST, SECOND)

    def gather_1(g):
        take_all(g, FIRST)
        send_all(g, FIRST_FAR, SECOND_PAIR)

    def gather_2(g):
        take_all(g, FIRST_FAR)
        send_all(g, SECOND_FAR)
        take_all(g, SECOND)
        send_all(g, OWN_ON)
        send_across(g, 0)

    def gather_3(g):
        take_all(g, SECOND_PAIR)
        send_all(g, PAIR_ON)

    def gather_4(g):
        take_all(g, SECOND_FAR)
        send_all(g, FAR_ON)
        send_across(g, 1, 2)

    def gather_5(g):
        take_all(g, OWN_ON, PAIR_ON, FAR_ON)
        send_across(g, 3)

    def gather_6(g):
        for number in range(4):
            for j in range(2):
                across_copy(g, j, number, True).wait_recv()

    def match(b):
        def body(i, carry):
            found, where = carry
            hit = renewed[i] == ids[b]
            return jnp.where(hit, 1, found), jnp.where(hit, i, where)

        return lax.fori_loop(0, renewed_hbm.shape[0], body, (jnp.int32(0), jnp.int32(0)))

    def chosen(held, cached, b, found, where):
        j, of_core, px, py = where % 2, (where // 2) % 2, (where // 4) % SIDE, where // 16
        second, first = jnp.where(j == 0, py, px), jnp.where(j == 0, px, py)
        return jnp.where(found > 0, held[line_of(j, second, of_core) + across_line(first)], cached[b])

    piece = rows // Z

    slice_half = piece // 4
    ADJACENT, THIRD, FOURTH, MERGED = range(4)

    def toward(direction, distance):
        return (z + distance * (1 - 2 * direction) + Z) % Z

    def half_of(direction):
        return pl.ds(direction * slice_half, slice_half)

    def part_copy(kind, direction):
        if kind == ADJACENT:
            src, distance = part_out.at[toward(direction, 1)], 1
        elif kind == THIRD:
            src, distance = part_out.at[toward(direction, 3)], 1
        elif kind == FOURTH:
            src, distance = part_out.at[toward(direction, 4), half_of(direction)], 2
        else:
            src, distance = merged.at[direction], 2
        dst = part_in.at[kind, direction]
        return pltpu.make_async_remote_copy(
            src_ref=src, dst_ref=dst.at[half_of(direction)] if kind == FOURTH else dst,
            send_sem=part_send.at[kind, direction], recv_sem=part_recv.at[kind, direction],
            device_id={"tensor": toward(direction, distance)}, device_id_type=pl.DeviceIdType.MESH,
        )

    def shrunk_copy(kind, direction):
        if kind < 2:
            src, dst, distance = shrunk.at[0], shrunk.at[(Z - 1 - kind) if direction else 1 + kind], 1 + kind
        elif kind == 2:
            src, dst, distance = shrunk.at[6 if direction else 2], shrunk.at[5 if direction else 3], 1
        else:
            spot = half_of(direction)
            src, dst, distance = shrunk.at[6 if direction else 2, spot], shrunk.at[4, spot], 2
        return pltpu.make_async_remote_copy(
            src_ref=src, dst_ref=dst,
            send_sem=shrunk_send.at[kind, direction], recv_sem=shrunk_recv.at[kind, direction],
            device_id={"tensor": toward(direction, distance)}, device_id_type=pl.DeviceIdType.MESH,
        )

    def shrink_parts(matches):
        for b in range(blocks):
            factor = chosen(every_a, cached_a, b, *matches[b])
            part = lax.dot_general(
                acts[pl.ds(b * TILE, TILE)], factor, (((1,), (1,)), ((), ())), preferred_element_type=F32
            )
            for q in range(TILE // piece):
                upper = part[q * piece : q * piece + piece // 2]
                lower = part[q * piece + piece // 2 : (q + 1) * piece]
                part_out[b * (TILE // piece) + q] = jnp.concatenate([upper, lower], axis=1).astype(BF16)
        for kind in (THIRD, FOURTH, ADJACENT):
            for direction in range(2):
                part_copy(kind, direction).start()

    def shrink_merge():
        for direction in range(2):
            part_copy(THIRD, direction).wait_recv()
            part_copy(FOURTH, direction).wait_recv()
            value = part_out[toward(direction, 2)].astype(F32) + part_in[THIRD, direction].astype(F32)
            spot = half_of(direction)
            rest = half_of(1 - direction)
            share = value[direction * slice_half : (direction + 1) * slice_half]
            merged[direction, spot] = (share + part_in[FOURTH, direction, spot].astype(F32)).astype(BF16)
            merged[direction, rest] = value[(1 - direction) * slice_half : (2 - direction) * slice_half].astype(BF16)
            part_copy(MERGED, direction).start()

    def shrink_sum():
        value = part_out[z].astype(F32)
        for kind in (ADJACENT, MERGED):
            for direction in range(2):
                part_copy(kind, direction).wait_recv()
                value = value + part_in[kind, direction].astype(F32)
        shrunk[0] = value.astype(BF16)
        for kind in (1, 0):
            for direction in range(2):
                shrunk_copy(kind, direction).start()

    def shrink_relay():
        for direction in range(2):
            shrunk_copy(1, direction).wait_recv()
            shrunk_copy(3, direction).start()
            shrunk_copy(2, direction).start()

    def expand(matches):
        for kind in (0, 2, 3):
            for direction in range(2):
                shrunk_copy(kind, direction).wait_recv()
        for b in range(blocks):
            factor = chosen(every_b, cached_b, b, *matches[b])
            lines = []
            for q in range(TILE // piece):
                packed = shrunk[(z + Z - b * (TILE // piece) - q) % Z].astype(F32)
                lines += [packed[:, :rank], packed[:, rank:]]
            lines = jnp.concatenate(lines, axis=0).astype(BF16)
            spot = pl.ds(b * TILE, TILE)
            total[spot] = total[spot] + adapter_scale * dot(lines, factor)

    def own_base():
        weight_load(0).wait()
        for i in range(rows // TILE):
            spot = pl.ds(i * TILE, TILE)
            total[spot] = dot(acts[spot], weight[0])

    def add_short():
        for direction, tile in ways:
            ring_copy(direction, LAST_SHORT, tile).wait_recv()
            spot = lines(direction, False, tile)
            total[spot] = total[spot] + incoming[direction, LAST_SHORT, pl.ds(tile * TILE, TILE)].astype(F32)

    def finish():
        size = TILE // PARTS
        for tile in range(tiles):
            for part in range(PARTS):
                for direction in range(2):
                    ring_copy(direction, LAST_LONG, tile, part, PARTS).wait_recv()
                    side = direction * half
                    spot = pl.ds(side + tile * TILE + part * size, size)
                    got = incoming[direction, LAST_LONG, pl.ds(tile * TILE + part * size, size)]
                    result[spot] = (total[spot] + got.astype(F32)).astype(BF16)

    def drain_gather(g):
        for kind in range(8):
            for j, direction in both:
                gather_copy(g, j, kind, direction).wait_send()
        for number in range(4):
            for j in range(2):
                across_copy(g, j, number).wait_send()

    def drain_ring(*slots):
        for slot in slots:
            parts = PARTS if slot == LAST_LONG else 1
            for direction, tile in ways:
                for part in range(parts):
                    ring_copy(direction, slot, tile, part, parts).wait_send()

    weight_load(4).wait()
    loads[0].wait()
    for direction in range(2):
        ring_piece(0, direction, 0)
    pl.semaphore_wait(barrier, Z - 1 + 5)
    for direction in range(2):
        ring_send_piece(0, direction, 0)
    for direction in range(2):
        for tile in range(1, tiles):
            ring_piece(0, direction, tile)
            ring_send_piece(0, direction, tile)
    gather_0(0)
    for i in (3, 5, 2, 6, 1, 7, 0):
        weight_load(i).start()
    for j in range(2):
        fresh_loads[1][j].start()
    for load in loads[1:]:
        load.start()
    ring_step(1)
    own_base()
    for load in loads[1:]:
        load.wait()
    matches = [match(b) for b in range(blocks)]
    gather_1(0)
    ring_step(2)
    gather_2(0)
    gather_3(0)
    ring_step(3)
    gather_4(0)
    gather_0(1)
    ring_step(4)
    gather_5(0)
    gather_1(1)
    gather_6(0)
    shrink_parts(matches)
    gather_2(1)
    weight_load(1).wait()
    weight_load(7).wait()
    ring_tile(5, 0)
    ring_tile(5, 1, False)
    shrink_merge()
    ring_out(5, 1)
    gather_3(1)
    gather_4(1)
    ring_tile(6, 0, False)
    shrink_sum()
    ring_out(6, 0)
    ring_tile(6, 1, False)
    gather_5(1)
    shrink_relay()
    ring_out(6, 1)
    gather_6(1)
    add_short()
    drain_gather(0)
    drain_gather(1)
    drain_ring(0, 1, 2, 3, 4, 5)
    expand(matches)
    for kind in range(4):
        for direction in range(2):
            part_copy(kind, direction).wait_send()
            shrunk_copy(kind, direction).wait_send()
    finish()
    drain_ring(6)


def shards(acts, weight, block_ids, cached_a, cached_b, renewed_module_numbers, fresh_a, renewed_second_matrices):
    rows, depth = acts.shape
    width = cached_b.shape[2]
    blocks, rank = cached_b.shape[0], cached_b.shape[1]
    tiles = rows // 2 // TILE
    slots = len(SLOTS)
    dma = pltpu.SemaphoreType.DMA
    return pl.pallas_call(
        kernel,
        out_shape=pltpu.VMEM((rows, width), BF16),
        in_specs=[pl.BlockSpec(memory_space=pl.ANY)] * 8,
        out_specs=pl.BlockSpec(memory_space=pltpu.VMEM),
        scratch_shapes=[
            pltpu.VMEM((rows, depth), BF16),
            pltpu.VMEM((Z, depth, width), BF16),
            pltpu.SMEM(block_ids.shape, jnp.int32),
            pltpu.SMEM(renewed_module_numbers.shape, jnp.int32),
            pltpu.VMEM((blocks, rank, depth), BF16),
            pltpu.VMEM((blocks, rank, width), BF16),
            pltpu.VMEM((2 * 2 * SIDE * SIDE, rank, depth), BF16),
            pltpu.VMEM((2 * 2 * SIDE * SIDE, rank, width), BF16),
            pltpu.VMEM((2, slots, rows // 2, width), BF16),
            pltpu.VMEM((2, slots, rows // 2, width), BF16),
            pltpu.VMEM((rows, width), F32),
            pltpu.VMEM((Z, rows // Z // 2, 2 * rank), BF16),
            pltpu.VMEM((4, 2, rows // Z // 2, 2 * rank), BF16),
            pltpu.VMEM((2, rows // Z // 2, 2 * rank), BF16),
            pltpu.VMEM((Z, rows // Z // 2, 2 * rank), BF16),
            dma((5,)),
            dma((Z,)),
            dma((2, 2)),
            dma((2, slots, tiles * PARTS)),
            dma((2, slots, tiles * PARTS)),
            dma((2, 2, 20)),
            dma((2, 2, 20)),
            dma((4, 2)),
            dma((4, 2)),
            dma((4, 2)),
            dma((4, 2)),
        ],
        compiler_params=pltpu.CompilerParams(
            collective_id=0, has_side_effects=True, vmem_limit_bytes=60 * 1024 * 1024
        ),
    )(
        acts, weight, block_ids, jnp.swapaxes(cached_a, 1, 2), cached_b,
        renewed_module_numbers, jnp.swapaxes(fresh_a, 1, 2), renewed_second_matrices,
    )


def solution(mesh):
    return jax.shard_map(
        shards,
        mesh=mesh,
        in_specs=(
            P("dp", "tensor"),
            P("tensor", None),
            P("dp"),
            P("dp", "tensor", None),
            P("dp", None, "tensor"),
            P(),
            P("dp", "tensor", None),
            P("dp", None, "tensor"),
        ),
        out_specs=P("dp", "tensor"),
        check_vma=False,
    )
```

```python
import jax
import jax.numpy as jnp
from jax import lax
from jax.experimental import pallas as pl
from jax.experimental.pallas import tpu as pltpu
from jax.sharding import PartitionSpec as P

adapter_scale = 2.0
Z = 8
SIDE = 4
TILE = 128
PARTS = 2
SHIFTED = (7, 4)
BF16 = jnp.bfloat16
F32 = jnp.float32

SLOTS = (
    (True, 0, None),
    (False, 1, None),
    (True, 1, 0),
    (False, 2, 1),
    (True, 2, 2),
    (False, 3, 3),
    (True, 3, 4),
)
LAST_LONG, LAST_SHORT = 6, 5

FIRST, SECOND, FIRST_FAR, SECOND_PAIR, SECOND_FAR, OWN_ON, PAIR_ON, FAR_ON = range(8)
ROWS_ACROSS = 16


def dot(a, b):
    return jnp.dot(a, b, preferred_element_type=F32)


def kernel(
    acts_hbm, weight_hbm, ids_hbm, cached_a_hbm, cached_b_hbm, renewed_hbm, fresh_a_hbm, fresh_b_hbm,
    result,
    acts, weight, ids, renewed, cached_a, cached_b, every_a, every_b,
    outgoing, incoming, strip_in, total, part_out, part_in, merged, shrunk,
    load_sem, weight_sem, fresh_sem,
    ring_send, ring_recv, strip_send, strip_recv, gather_send, gather_recv, part_send, part_recv, shrunk_send, shrunk_recv,
):
    z = lax.axis_index("tensor")
    dp = lax.axis_index("dp")
    core = dp % 2
    x = (dp // 2) % SIDE
    y = dp // (2 * SIDE)
    depth, width = weight.shape[1], weight.shape[2]
    blocks = ids_hbm.shape[0]
    rows = acts.shape[0]
    half = rows // 2
    tiles = half // TILE
    rank = cached_a.shape[1]

    def at_xy(px, py, pc):
        return {"dp": (py * SIDE + px) * 2 + pc}

    def along(axis, step):
        if axis == 0:
            return at_xy((x + step + SIDE) % SIDE, y, core)
        return at_xy(x, (y + step + SIDE) % SIDE, core)

    sibling = at_xy(x, y, 1 - core)

    def weight_load(i):
        column = pl.multiple_of((z + i) % Z * width, 128)
        return pltpu.make_async_copy(weight_hbm.at[:, pl.ds(column, width)], weight.at[i], weight_sem.at[i])

    loads = [
        pltpu.make_async_copy(acts_hbm, acts, load_sem.at[0]),
        pltpu.make_async_copy(cached_a_hbm, cached_a, load_sem.at[1]),
        pltpu.make_async_copy(cached_b_hbm, cached_b, load_sem.at[2]),
        pltpu.make_async_copy(ids_hbm, ids, load_sem.at[3]),
        pltpu.make_async_copy(renewed_hbm, renewed, load_sem.at[4]),
    ]
    mine = (
        (core * SIDE + y) * SIDE + (x % 2) * 2 + x // 2,
        ((2 + core) * SIDE + x) * SIDE + (y % 2) * 2 + y // 2,
    )
    gathers = ((every_a, fresh_a_hbm), (every_b, fresh_b_hbm))
    fresh_loads = [
        [pltpu.make_async_copy(source.at[j], held.at[mine[j]], fresh_sem.at[g, j]) for j in range(2)]
        for g, (held, source) in enumerate(gathers)
    ]

    barrier = pltpu.get_barrier_semaphore()
    for i in (1, Z - 1):
        pl.semaphore_signal(barrier, inc=1, device_id={"tensor": (z + i) % Z}, device_id_type=pl.DeviceIdType.MESH)
    for axis in range(2):
        for step in (1, -1):
            pl.semaphore_signal(barrier, inc=1, device_id=along(axis, step), device_id_type=pl.DeviceIdType.MESH)
    pl.semaphore_signal(barrier, inc=1, device_id=sibling, device_id_type=pl.DeviceIdType.MESH)

    weight_load(4).start()
    loads[0].start()
    for j in range(2):
        fresh_loads[0][j].start()

    def ring_copy(direction, slot, tile, part=0, parts=1):
        spot = pl.ds(tile * TILE + part * (TILE // parts), TILE // parts)
        return pltpu.make_async_remote_copy(
            src_ref=outgoing.at[direction, slot, spot],
            dst_ref=incoming.at[direction, slot, spot],
            send_sem=ring_send.at[direction, slot, tile * PARTS + part],
            recv_sem=ring_recv.at[direction, slot, tile * PARTS + part],
            device_id={"tensor": (z + 1 - 2 * direction + Z) % Z},
            device_id_type=pl.DeviceIdType.MESH,
        )

    ways = [(direction, tile) for tile in range(tiles) for direction in range(2)]

    def lines(direction, is_long, tile):
        side = direction if is_long else 1 - direction
        return pl.ds(side * half + tile * TILE, TILE)

    strip = pl.ds(half - TILE // PARTS, TILE // PARTS)

    def parts_of(slot, tile):
        return PARTS if slot == LAST_LONG or (slot < 2 and tile == tiles - 1) else 1

    def copies_of(slot, direction, tile):
        parts = parts_of(slot, tile)
        return [ring_copy(direction, slot, tile, part, parts) for part in range(parts)]

    def strip_other(direction):
        return pltpu.make_async_remote_copy(
            src_ref=outgoing.at[1 - direction, 0, strip],
            dst_ref=strip_in.at[direction],
            send_sem=strip_send.at[direction],
            recv_sem=strip_recv.at[direction],
            device_id={"tensor": (z + 1 - 2 * direction + Z) % Z},
            device_id_type=pl.DeviceIdType.MESH,
        )

    def before_me(direction):
        return (z - 1 + 2 * direction + Z) % Z

    def ring_piece(slot, direction, tile):
        is_long, step, before = SLOTS[slot]
        spot = pl.ds(tile * TILE, TILE)
        term = dot(acts[lines(direction, is_long, tile)], weight[4 - step + 2 * step * direction])
        if before == 0 and tile == tiles - 1:
            first = pl.ds(tile * TILE, TILE // PARTS)
            kept, ends = copies_of(0, direction, tile)
            kept.wait_recv()
            upper = term[: TILE // PARTS] + incoming[direction, 0, first].astype(F32)
            outgoing[direction, slot, first] = upper.astype(BF16)
            outgoing[direction, slot, strip] = term[TILE // PARTS :].astype(BF16)

            @pl.when(before_me(direction) != SHIFTED[direction])
            def _():
                ends.wait_recv()
                lower = outgoing[direction, slot, strip].astype(F32) + incoming[direction, 0, strip].astype(F32)
                outgoing[direction, slot, strip] = lower.astype(BF16)

            return
        if before is not None:
            for copy in copies_of(before, direction, tile):
                copy.wait_recv()
            term = term + incoming[direction, before, spot].astype(F32)
        outgoing[direction, slot, spot] = term.astype(BF16)

    def ring_send_piece(slot, direction, tile):
        copies = copies_of(slot, direction, tile)
        if slot < 2 and tile == tiles - 1:
            copies[0].start()
            if slot == 0:
                pl.when(z != SHIFTED[direction])(copies[1].start)
            return
        for copy in copies:
            copy.start()

    def strips_away():
        for direction in range(2):
            pl.when(z == SHIFTED[1 - direction])(strip_other(direction).start)

    def strips_on():
        for direction in range(2):

            @pl.when(before_me(direction) == SHIFTED[1 - direction])
            def _():
                strip_other(direction).wait_recv()
                value = outgoing[direction, 1, strip].astype(F32) + strip_in[direction].astype(F32)
                outgoing[direction, 1, strip] = value.astype(BF16)

            copies_of(1, direction, tiles - 1)[1].start()

    def ring_step(slot):
        is_long, step, _ = SLOTS[slot]
        if not is_long:
            weight_load(4 - step).wait()
            weight_load(4 + step).wait()
        for tile in range(tiles):
            ring_tile(slot, tile)

    def ring_tile(slot, tile, send=True):
        for direction in range(2):
            ring_piece(slot, direction, tile)
            if send:
                ring_send_piece(slot, direction, tile)

    def ring_out(slot, tile):
        for direction in range(2):
            ring_send_piece(slot, direction, tile)

    def line_of(j, second, of_core):
        return ((j * 2 + of_core) * SIDE + second) * SIDE

    def across_line(first):
        return (first % 2) * 2 + first // 2

    def gather_copy(g, j, kind, direction=0, incoming_side=False):
        held = gathers[g][0]
        first, second = (x, y) if j == 0 else (y, x)
        first_axis, second_axis = (0, 1) if j == 0 else (1, 0)
        sign = 1 - 2 * direction
        back = -sign if incoming_side else 0
        here = across_line(first)
        pair = (1 - first % 2) * 2
        far = across_line((first + 2) % SIDE)
        part = pl.ds(direction * (rank // 2), rank // 2)

        def line(step):
            return line_of(j, (second + step + SIDE) % SIDE, core)

        axis = second_axis
        if kind == FIRST:
            axis = first_axis
            ref = held.at[line(0) + across_line((first + back + SIDE) % SIDE)]
        elif kind == FIRST_FAR:
            axis = first_axis
            ref = held.at[line(0) + across_line((first + back - sign + SIDE) % SIDE), part]
        elif kind == SECOND:
            ref = held.at[line(back) + here]
        elif kind == SECOND_PAIR:
            ref = held.at[pl.ds(line(back) + pair, 2)]
        elif kind == SECOND_FAR:
            ref = held.at[line(back) + far]
        elif kind == OWN_ON:
            ref = held.at[line(back - sign) + here, part]
        elif kind == PAIR_ON:
            ref = held.at[line(back - sign) + pair + direction]
        else:
            ref = held.at[line(back - sign) + far, part]
        number = 2 * kind + direction
        return pltpu.make_async_remote_copy(
            src_ref=ref, dst_ref=ref,
            send_sem=gather_send.at[g, j, number], recv_sem=gather_recv.at[g, j, number],
            device_id=along(axis, sign), device_id_type=pl.DeviceIdType.MESH,
        )

    def across_copy(g, j, number, incoming_side=False):
        held = gathers[g][0]
        second = y if j == 0 else x
        moved = (second + (0, -1, 1, 2)[number] + SIDE) % SIDE
        ref = held.at[pl.ds(line_of(j, moved, 1 - core if incoming_side else core), SIDE)]
        return pltpu.make_async_remote_copy(
            src_ref=ref, dst_ref=ref,
            send_sem=gather_send.at[g, j, ROWS_ACROSS + number], recv_sem=gather_recv.at[g, j, ROWS_ACROSS + number],
            device_id=sibling, device_id_type=pl.DeviceIdType.MESH,
        )

    both = [(j, direction) for j in range(2) for direction in range(2)]

    def send_all(g, *kinds):
        for kind in kinds:
            for j, direction in both:
                gather_copy(g, j, kind, direction).start()

    def take_all(g, *kinds):
        for kind in kinds:
            for j, direction in both:
                gather_copy(g, j, kind, direction, True).wait_recv()

    def send_across(g, *numbers):
        for number in numbers:
            for j in range(2):
                across_copy(g, j, number).start()

    def gather_0(g):
        for j in range(2):
            fresh_loads[g][j].wait()
        send_all(g, FIRST, SECOND)

    def gather_1(g):
        take_all(g, FIRST)
        send_all(g, FIRST_FAR, SECOND_PAIR)

    def gather_2(g):
        take_all(g, FIRST_FAR)
        send_all(g, SECOND_FAR)
        take_all(g, SECOND)
        send_all(g, OWN_ON)
        send_across(g, 0)

    def gather_3(g):
        take_all(g, SECOND_PAIR)
        send_all(g, PAIR_ON)

    def gather_4(g):
        take_all(g, SECOND_FAR)
        send_all(g, FAR_ON)
        send_across(g, 1, 2)

    def gather_5(g):
        take_all(g, OWN_ON, PAIR_ON, FAR_ON)
        send_across(g, 3)

    def gather_6(g):
        for number in range(4):
            for j in range(2):
                across_copy(g, j, number, True).wait_recv()

    def match(b):
        def body(i, carry):
            found, where = carry
            hit = renewed[i] == ids[b]
            return jnp.where(hit, 1, found), jnp.where(hit, i, where)

        return lax.fori_loop(0, renewed_hbm.shape[0], body, (jnp.int32(0), jnp.int32(0)))

    def chosen(held, cached, b, found, where):
        j, of_core, px, py = where % 2, (where // 2) % 2, (where // 4) % SIDE, where // 16
        second, first = jnp.where(j == 0, py, px), jnp.where(j == 0, px, py)
        return jnp.where(found > 0, held[line_of(j, second, of_core) + across_line(first)], cached[b])

    piece = rows // Z

    slice_half = piece // 4
    ADJACENT, THIRD, FOURTH, MERGED = range(4)

    def toward(direction, distance):
        return (z + distance * (1 - 2 * direction) + Z) % Z

    def half_of(direction):
        return pl.ds(direction * slice_half, slice_half)

    def part_copy(kind, direction):
        if kind == ADJACENT:
            src, distance = part_out.at[toward(direction, 1)], 1
        elif kind == THIRD:
            src, distance = part_out.at[toward(direction, 3)], 1
        elif kind == FOURTH:
            src, distance = part_out.at[toward(direction, 4), half_of(direction)], 2
        else:
            src, distance = merged.at[direction], 2
        dst = part_in.at[kind, direction]
        return pltpu.make_async_remote_copy(
            src_ref=src, dst_ref=dst.at[half_of(direction)] if kind == FOURTH else dst,
            send_sem=part_send.at[kind, direction], recv_sem=part_recv.at[kind, direction],
            device_id={"tensor": toward(direction, distance)}, device_id_type=pl.DeviceIdType.MESH,
        )

    def shrunk_copy(kind, direction):
        if kind < 2:
            src, dst, distance = shrunk.at[0], shrunk.at[(Z - 1 - kind) if direction else 1 + kind], 1 + kind
        elif kind == 2:
            src, dst, distance = shrunk.at[6 if direction else 2], shrunk.at[5 if direction else 3], 1
        else:
            spot = half_of(direction)
            src, dst, distance = shrunk.at[6 if direction else 2, spot], shrunk.at[4, spot], 2
        return pltpu.make_async_remote_copy(
            src_ref=src, dst_ref=dst,
            send_sem=shrunk_send.at[kind, direction], recv_sem=shrunk_recv.at[kind, direction],
            device_id={"tensor": toward(direction, distance)}, device_id_type=pl.DeviceIdType.MESH,
        )

    def shrink_parts(matches):
        for b in range(blocks):
            factor = chosen(every_a, cached_a, b, *matches[b])
            part = lax.dot_general(
                acts[pl.ds(b * TILE, TILE)], factor, (((1,), (1,)), ((), ())), preferred_element_type=F32
            )
            for q in range(TILE // piece):
                upper = part[q * piece : q * piece + piece // 2]
                lower = part[q * piece + piece // 2 : (q + 1) * piece]
                part_out[b * (TILE // piece) + q] = jnp.concatenate([upper, lower], axis=1).astype(BF16)
        for kind in (THIRD, FOURTH, ADJACENT):
            for direction in range(2):
                part_copy(kind, direction).start()

    def shrink_merge():
        for direction in range(2):
            part_copy(THIRD, direction).wait_recv()
            part_copy(FOURTH, direction).wait_recv()
            value = part_out[toward(direction, 2)].astype(F32) + part_in[THIRD, direction].astype(F32)
            spot = half_of(direction)
            rest = half_of(1 - direction)
            share = value[direction * slice_half : (direction + 1) * slice_half]
            merged[direction, spot] = (share + part_in[FOURTH, direction, spot].astype(F32)).astype(BF16)
            merged[direction, rest] = value[(1 - direction) * slice_half : (2 - direction) * slice_half].astype(BF16)
            part_copy(MERGED, direction).start()

    def shrink_sum():
        value = part_out[z].astype(F32)
        for kind in (ADJACENT, MERGED):
            for direction in range(2):
                part_copy(kind, direction).wait_recv()
                value = value + part_in[kind, direction].astype(F32)
        shrunk[0] = value.astype(BF16)
        for kind in (1, 0):
            for direction in range(2):
                shrunk_copy(kind, direction).start()

    def shrink_relay():
        for direction in range(2):
            shrunk_copy(1, direction).wait_recv()
            shrunk_copy(3, direction).start()
            shrunk_copy(2, direction).start()

    def expand(matches):
        for kind in (0, 2, 3):
            for direction in range(2):
                shrunk_copy(kind, direction).wait_recv()
        for b in range(blocks):
            factor = chosen(every_b, cached_b, b, *matches[b])
            lines = []
            for q in range(TILE // piece):
                packed = shrunk[(z + Z - b * (TILE // piece) - q) % Z].astype(F32)
                lines += [packed[:, :rank], packed[:, rank:]]
            lines = jnp.concatenate(lines, axis=0).astype(BF16)
            spot = pl.ds(b * TILE, TILE)
            total[spot] = total[spot] + adapter_scale * dot(lines, factor)

    def own_base():
        weight_load(0).wait()
        for i in range(rows // TILE):
            spot = pl.ds(i * TILE, TILE)
            total[spot] = dot(acts[spot], weight[0])

    def add_short():
        for direction, tile in ways:
            ring_copy(direction, LAST_SHORT, tile).wait_recv()
            spot = lines(direction, False, tile)
            total[spot] = total[spot] + incoming[direction, LAST_SHORT, pl.ds(tile * TILE, TILE)].astype(F32)

    def finish():
        size = TILE // PARTS
        for tile in range(tiles):
            for part in range(PARTS):
                for direction in range(2):
                    ring_copy(direction, LAST_LONG, tile, part, PARTS).wait_recv()
                    side = direction * half
                    spot = pl.ds(side + tile * TILE + part * size, size)
                    got = incoming[direction, LAST_LONG, pl.ds(tile * TILE + part * size, size)]
                    result[spot] = (total[spot] + got.astype(F32)).astype(BF16)

    def drain_gather(g):
        for kind in range(8):
            for j, direction in both:
                gather_copy(g, j, kind, direction).wait_send()
        for number in range(4):
            for j in range(2):
                across_copy(g, j, number).wait_send()

    def drain_ring(*slots):
        for slot in slots:
            for direction, tile in ways:
                copies = copies_of(slot, direction, tile)
                if slot == 0 and tile == tiles - 1:
                    copies[0].wait_send()
                    pl.when(z != SHIFTED[direction])(copies[1].wait_send)
                    pl.when(z == SHIFTED[1 - direction])(strip_other(direction).wait_send)
                    continue
                for copy in copies:
                    copy.wait_send()

    weight_load(4).wait()
    loads[0].wait()
    for direction in range(2):
        ring_piece(0, direction, 0)
    pl.semaphore_wait(barrier, 7)
    for direction in range(2):
        ring_send_piece(0, direction, 0)
    for direction in range(2):
        for tile in range(1, tiles):
            ring_piece(0, direction, tile)
            ring_send_piece(0, direction, tile)
    strips_away()
    gather_0(0)
    for i in (3, 5, 2, 6, 1, 7, 0):
        weight_load(i).start()
    for j in range(2):
        fresh_loads[1][j].start()
    for load in loads[1:]:
        load.start()
    ring_step(1)
    own_base()
    for load in loads[1:]:
        load.wait()
    matches = [match(b) for b in range(blocks)]
    gather_1(0)
    ring_step(2)
    strips_on()
    gather_2(0)
    gather_3(0)
    ring_step(3)
    gather_4(0)
    gather_0(1)
    ring_step(4)
    gather_5(0)
    gather_1(1)
    gather_6(0)
    shrink_parts(matches)
    gather_2(1)
    weight_load(1).wait()
    weight_load(7).wait()
    ring_tile(5, 0)
    ring_tile(5, 1, False)
    shrink_merge()
    ring_out(5, 1)
    gather_3(1)
    gather_4(1)
    ring_tile(6, 0, False)
    shrink_sum()
    ring_out(6, 0)
    ring_tile(6, 1, False)
    gather_5(1)
    shrink_relay()
    ring_out(6, 1)
    gather_6(1)
    add_short()
    drain_gather(0)
    drain_gather(1)
    drain_ring(0, 1, 2, 3, 4, 5)
    expand(matches)
    for kind in range(4):
        for direction in range(2):
            part_copy(kind, direction).wait_send()
            shrunk_copy(kind, direction).wait_send()
    finish()
    drain_ring(6)


def shards(acts, weight, block_ids, cached_a, cached_b, renewed_module_numbers, fresh_a, renewed_second_matrices):
    rows, depth = acts.shape
    width = cached_b.shape[2]
    blocks, rank = cached_b.shape[0], cached_b.shape[1]
    tiles = rows // 2 // TILE
    slots = len(SLOTS)
    dma = pltpu.SemaphoreType.DMA
    return pl.pallas_call(
        kernel,
        out_shape=pltpu.VMEM((rows, width), BF16),
        in_specs=[pl.BlockSpec(memory_space=pl.ANY)] * 8,
        out_specs=pl.BlockSpec(memory_space=pltpu.VMEM),
        scratch_shapes=[
            pltpu.VMEM((rows, depth), BF16),
            pltpu.VMEM((Z, depth, width), BF16),
            pltpu.SMEM(block_ids.shape, jnp.int32),
            pltpu.SMEM(renewed_module_numbers.shape, jnp.int32),
            pltpu.VMEM((blocks, rank, depth), BF16),
            pltpu.VMEM((blocks, rank, width), BF16),
            pltpu.VMEM((2 * 2 * SIDE * SIDE, rank, depth), BF16),
            pltpu.VMEM((2 * 2 * SIDE * SIDE, rank, width), BF16),
            pltpu.VMEM((2, slots, rows // 2, width), BF16),
            pltpu.VMEM((2, slots, rows // 2, width), BF16),
            pltpu.VMEM((2, TILE // PARTS, width), BF16),
            pltpu.VMEM((rows, width), F32),
            pltpu.VMEM((Z, rows // Z // 2, 2 * rank), BF16),
            pltpu.VMEM((4, 2, rows // Z // 2, 2 * rank), BF16),
            pltpu.VMEM((2, rows // Z // 2, 2 * rank), BF16),
            pltpu.VMEM((Z, rows // Z // 2, 2 * rank), BF16),
            dma((5,)),
            dma((Z,)),
            dma((2, 2)),
            dma((2, slots, tiles * PARTS)),
            dma((2, slots, tiles * PARTS)),
            dma((2,)),
            dma((2,)),
            dma((2, 2, 20)),
            dma((2, 2, 20)),
            dma((4, 2)),
            dma((4, 2)),
            dma((4, 2)),
            dma((4, 2)),
        ],
        compiler_params=pltpu.CompilerParams(
            collective_id=0, has_side_effects=True, vmem_limit_bytes=60 * 1024 * 1024
        ),
    )(
        acts, weight, block_ids, jnp.swapaxes(cached_a, 1, 2), cached_b,
        renewed_module_numbers, jnp.swapaxes(fresh_a, 1, 2), renewed_second_matrices,
    )


def solution(mesh):
    return jax.shard_map(
        shards,
        mesh=mesh,
        in_specs=(
            P("dp", "tensor"),
            P("tensor", None),
            P("dp"),
            P("dp", "tensor", None),
            P("dp", None, "tensor"),
            P(),
            P("dp", "tensor", None),
            P("dp", None, "tensor"),
        ),
        out_specs=P("dp", "tensor"),
        check_vma=False,
    )
```

```python
import jax
import jax.numpy as jnp
from jax import lax
from jax.experimental import pallas as pl
from jax.experimental.pallas import tpu as pltpu
from jax.sharding import PartitionSpec as P

adapter_scale = 2.0
Z = 8
SIDE = 4
TILE = 128
PARTS = 2
SHIFTED = (7, 4)
BF16 = jnp.bfloat16
F32 = jnp.float32

SLOTS = (
    (True, 0, None),
    (False, 1, None),
    (True, 1, 0),
    (False, 2, 1),
    (True, 2, 2),
    (False, 3, 3),
    (True, 3, 4),
)
LAST_LONG, LAST_SHORT = 6, 5

FIRST, SECOND, FIRST_FAR, SECOND_PAIR, SECOND_FAR, OWN_ON, PAIR_ON, FAR_ON = range(8)
ROWS_ACROSS = 16


def dot(a, b):
    return jnp.dot(a, b, preferred_element_type=F32)


def kernel(
    acts_hbm, weight_hbm, ids_hbm, cached_a_hbm, cached_b_hbm, renewed_hbm, fresh_a_hbm, fresh_b_hbm,
    result,
    acts, weight, ids, renewed, cached_a, cached_b, every_a, every_b,
    outgoing, incoming, strip_in, total, part_out, part_in, merged, shrunk,
    load_sem, weight_sem, fresh_sem,
    ring_send, ring_recv, strip_send, strip_recv, gather_send, gather_recv, part_send, part_recv, shrunk_send, shrunk_recv,
):
    z = lax.axis_index("tensor")
    dp = lax.axis_index("dp")
    core = dp % 2
    x = (dp // 2) % SIDE
    y = dp // (2 * SIDE)
    depth, width = weight.shape[1], weight.shape[2]
    blocks = ids_hbm.shape[0]
    rows = acts.shape[0]
    half = rows // 2
    tiles = half // TILE
    rank = cached_a.shape[1]

    def at_xy(px, py, pc):
        return {"dp": (py * SIDE + px) * 2 + pc}

    def along(axis, step):
        if axis == 0:
            return at_xy((x + step + SIDE) % SIDE, y, core)
        return at_xy(x, (y + step + SIDE) % SIDE, core)

    sibling = at_xy(x, y, 1 - core)

    def weight_load(i):
        column = pl.multiple_of((z + i) % Z * width, 128)
        return pltpu.make_async_copy(weight_hbm.at[:, pl.ds(column, width)], weight.at[i], weight_sem.at[i])

    loads = [
        pltpu.make_async_copy(acts_hbm, acts, load_sem.at[0]),
        pltpu.make_async_copy(cached_a_hbm, cached_a, load_sem.at[1]),
        pltpu.make_async_copy(cached_b_hbm, cached_b, load_sem.at[2]),
        pltpu.make_async_copy(ids_hbm, ids, load_sem.at[3]),
        pltpu.make_async_copy(renewed_hbm, renewed, load_sem.at[4]),
    ]
    mine = (
        (core * SIDE + y) * SIDE + (x % 2) * 2 + x // 2,
        ((2 + core) * SIDE + x) * SIDE + (y % 2) * 2 + y // 2,
    )
    gathers = ((every_a, fresh_a_hbm), (every_b, fresh_b_hbm))
    fresh_loads = [
        [pltpu.make_async_copy(source.at[j], held.at[mine[j]], fresh_sem.at[g, j]) for j in range(2)]
        for g, (held, source) in enumerate(gathers)
    ]

    barrier = pltpu.get_barrier_semaphore()
    for i in (1, Z - 1):
        pl.semaphore_signal(barrier, inc=1, device_id={"tensor": (z + i) % Z}, device_id_type=pl.DeviceIdType.MESH)
    for axis in range(2):
        for step in (1, -1):
            pl.semaphore_signal(barrier, inc=1, device_id=along(axis, step), device_id_type=pl.DeviceIdType.MESH)
    pl.semaphore_signal(barrier, inc=1, device_id=sibling, device_id_type=pl.DeviceIdType.MESH)

    weight_load(4).start()
    loads[0].start()
    for j in range(2):
        fresh_loads[0][j].start()

    def ring_copy(direction, slot, tile, part=0, parts=1):
        spot = pl.ds(tile * TILE + part * (TILE // parts), TILE // parts)
        return pltpu.make_async_remote_copy(
            src_ref=outgoing.at[direction, slot, spot],
            dst_ref=incoming.at[direction, slot, spot],
            send_sem=ring_send.at[direction, slot, tile * PARTS + part],
            recv_sem=ring_recv.at[direction, slot, tile * PARTS + part],
            device_id={"tensor": (z + 1 - 2 * direction + Z) % Z},
            device_id_type=pl.DeviceIdType.MESH,
        )

    ways = [(direction, tile) for tile in range(tiles) for direction in range(2)]

    def lines(direction, is_long, tile):
        side = direction if is_long else 1 - direction
        return pl.ds(side * half + tile * TILE, TILE)

    strip = pl.ds(half - TILE // PARTS, TILE // PARTS)

    def parts_of(slot, tile):
        return PARTS if slot == LAST_LONG or (slot < 2 and tile == tiles - 1) else 1

    def copies_of(slot, direction, tile):
        parts = parts_of(slot, tile)
        return [ring_copy(direction, slot, tile, part, parts) for part in range(parts)]

    def strip_other(direction):
        return pltpu.make_async_remote_copy(
            src_ref=outgoing.at[1 - direction, 0, strip],
            dst_ref=strip_in.at[direction],
            send_sem=strip_send.at[direction],
            recv_sem=strip_recv.at[direction],
            device_id={"tensor": (z + 1 - 2 * direction + Z) % Z},
            device_id_type=pl.DeviceIdType.MESH,
        )

    def before_me(direction):
        return (z - 1 + 2 * direction + Z) % Z

    def ring_piece(slot, direction, tile):
        is_long, step, before = SLOTS[slot]
        spot = pl.ds(tile * TILE, TILE)
        term = dot(acts[lines(direction, is_long, tile)], weight[4 - step + 2 * step * direction])
        if before == 0 and tile == tiles - 1:
            first = pl.ds(tile * TILE, TILE // PARTS)
            kept, ends = copies_of(0, direction, tile)
            kept.wait_recv()
            upper = term[: TILE // PARTS] + incoming[direction, 0, first].astype(F32)
            outgoing[direction, slot, first] = upper.astype(BF16)
            outgoing[direction, slot, strip] = term[TILE // PARTS :].astype(BF16)

            @pl.when(before_me(direction) != SHIFTED[direction])
            def _():
                ends.wait_recv()
                lower = outgoing[direction, slot, strip].astype(F32) + incoming[direction, 0, strip].astype(F32)
                outgoing[direction, slot, strip] = lower.astype(BF16)

            return
        if before is not None:
            for copy in copies_of(before, direction, tile):
                copy.wait_recv()
            term = term + incoming[direction, before, spot].astype(F32)
        outgoing[direction, slot, spot] = term.astype(BF16)

    def ring_send_piece(slot, direction, tile):
        copies = copies_of(slot, direction, tile)
        if slot < 2 and tile == tiles - 1:
            copies[0].start()
            if slot == 0:
                pl.when(z != SHIFTED[direction])(copies[1].start)
            return
        for copy in copies:
            copy.start()

    def strips_away():
        for direction in range(2):
            pl.when(z == SHIFTED[1 - direction])(strip_other(direction).start)

    def strips_on():
        for direction in range(2):

            @pl.when(before_me(direction) == SHIFTED[1 - direction])
            def _():
                strip_other(direction).wait_recv()
                value = outgoing[direction, 1, strip].astype(F32) + strip_in[direction].astype(F32)
                outgoing[direction, 1, strip] = value.astype(BF16)

            copies_of(1, direction, tiles - 1)[1].start()

    def ring_step(slot):
        is_long, step, _ = SLOTS[slot]
        if not is_long:
            weight_load(4 - step).wait()
            weight_load(4 + step).wait()
        for tile in range(tiles):
            ring_tile(slot, tile)

    def ring_tile(slot, tile, send=True):
        for direction in range(2):
            ring_piece(slot, direction, tile)
            if send:
                ring_send_piece(slot, direction, tile)

    def ring_out(slot, tile):
        for direction in range(2):
            ring_send_piece(slot, direction, tile)

    def line_of(j, second, of_core):
        return ((j * 2 + of_core) * SIDE + second) * SIDE

    def across_line(first):
        return (first % 2) * 2 + first // 2

    def gather_copy(g, j, kind, direction=0, incoming_side=False):
        held = gathers[g][0]
        first, second = (x, y) if j == 0 else (y, x)
        first_axis, second_axis = (0, 1) if j == 0 else (1, 0)
        sign = 1 - 2 * direction
        back = -sign if incoming_side else 0
        here = across_line(first)
        pair = (1 - first % 2) * 2
        far = across_line((first + 2) % SIDE)
        part = pl.ds(direction * (rank // 2), rank // 2)

        def line(step):
            return line_of(j, (second + step + SIDE) % SIDE, core)

        axis = second_axis
        if kind == FIRST:
            axis = first_axis
            ref = held.at[line(0) + across_line((first + back + SIDE) % SIDE)]
        elif kind == FIRST_FAR:
            axis = first_axis
            ref = held.at[line(0) + across_line((first + back - sign + SIDE) % SIDE), part]
        elif kind == SECOND:
            ref = held.at[line(back) + here]
        elif kind == SECOND_PAIR:
            ref = held.at[pl.ds(line(back) + pair, 2)]
        elif kind == SECOND_FAR:
            ref = held.at[line(back) + far]
        elif kind == OWN_ON:
            ref = held.at[line(back - sign) + here, part]
        elif kind == PAIR_ON:
            ref = held.at[line(back - sign) + pair + direction]
        else:
            ref = held.at[line(back - sign) + far, part]
        number = 2 * kind + direction
        return pltpu.make_async_remote_copy(
            src_ref=ref, dst_ref=ref,
            send_sem=gather_send.at[g, j, number], recv_sem=gather_recv.at[g, j, number],
            device_id=along(axis, sign), device_id_type=pl.DeviceIdType.MESH,
        )

    def across_copy(g, j, number, incoming_side=False):
        held = gathers[g][0]
        second = y if j == 0 else x
        moved = (second + (0, -1, 1, 2)[number] + SIDE) % SIDE
        ref = held.at[pl.ds(line_of(j, moved, 1 - core if incoming_side else core), SIDE)]
        return pltpu.make_async_remote_copy(
            src_ref=ref, dst_ref=ref,
            send_sem=gather_send.at[g, j, ROWS_ACROSS + number], recv_sem=gather_recv.at[g, j, ROWS_ACROSS + number],
            device_id=sibling, device_id_type=pl.DeviceIdType.MESH,
        )

    both = [(j, direction) for j in range(2) for direction in range(2)]

    def send_all(g, *kinds):
        for kind in kinds:
            for j, direction in both:
                gather_copy(g, j, kind, direction).start()

    def take_all(g, *kinds):
        for kind in kinds:
            for j, direction in both:
                gather_copy(g, j, kind, direction, True).wait_recv()

    def send_across(g, *numbers):
        for number in numbers:
            for j in range(2):
                across_copy(g, j, number).start()

    def gather_0(g):
        for j in range(2):
            fresh_loads[g][j].wait()
        send_all(g, FIRST, SECOND)

    def gather_1(g):
        take_all(g, FIRST)
        send_all(g, FIRST_FAR, SECOND_PAIR)

    def gather_2(g):
        take_all(g, FIRST_FAR)
        send_all(g, SECOND_FAR)
        take_all(g, SECOND)
        send_all(g, OWN_ON)
        send_across(g, 0)

    def gather_3(g):
        take_all(g, SECOND_PAIR)
        send_all(g, PAIR_ON)

    def gather_4(g):
        take_all(g, SECOND_FAR)
        send_all(g, FAR_ON)
        send_across(g, 1, 2)

    def gather_5(g):
        take_all(g, OWN_ON, PAIR_ON, FAR_ON)
        send_across(g, 3)

    def gather_6(g):
        for number in range(4):
            for j in range(2):
                across_copy(g, j, number, True).wait_recv()

    def match(b):
        def body(i, carry):
            found, where = carry
            hit = renewed[i] == ids[b]
            return jnp.where(hit, 1, found), jnp.where(hit, i, where)

        return lax.fori_loop(0, renewed_hbm.shape[0], body, (jnp.int32(0), jnp.int32(0)))

    def chosen(held, cached, b, found, where):
        j, of_core, px, py = where % 2, (where // 2) % 2, (where // 4) % SIDE, where // 16
        second, first = jnp.where(j == 0, py, px), jnp.where(j == 0, px, py)
        return jnp.where(found > 0, held[line_of(j, second, of_core) + across_line(first)], cached[b])

    piece = rows // Z

    slice_half = piece // 4
    ADJACENT, THIRD, FOURTH, MERGED = range(4)

    def toward(direction, distance):
        return (z + distance * (1 - 2 * direction) + Z) % Z

    def half_of(direction):
        return pl.ds(direction * slice_half, slice_half)

    def part_copy(kind, direction):
        if kind == ADJACENT:
            src, distance = part_out.at[toward(direction, 1)], 1
        elif kind == THIRD:
            src, distance = part_out.at[toward(direction, 3)], 1
        elif kind == FOURTH:
            src, distance = part_out.at[toward(direction, 4), half_of(direction)], 2
        else:
            src, distance = merged.at[direction], 2
        dst = part_in.at[kind, direction]
        return pltpu.make_async_remote_copy(
            src_ref=src, dst_ref=dst.at[half_of(direction)] if kind == FOURTH else dst,
            send_sem=part_send.at[kind, direction], recv_sem=part_recv.at[kind, direction],
            device_id={"tensor": toward(direction, distance)}, device_id_type=pl.DeviceIdType.MESH,
        )

    def shrunk_copy(kind, direction):
        if kind < 2:
            src, dst, distance = shrunk.at[0], shrunk.at[(Z - 1 - kind) if direction else 1 + kind], 1 + kind
        elif kind == 2:
            src, dst, distance = shrunk.at[6 if direction else 2], shrunk.at[5 if direction else 3], 1
        else:
            spot = half_of(direction)
            src, dst, distance = shrunk.at[6 if direction else 2, spot], shrunk.at[4, spot], 2
        return pltpu.make_async_remote_copy(
            src_ref=src, dst_ref=dst,
            send_sem=shrunk_send.at[kind, direction], recv_sem=shrunk_recv.at[kind, direction],
            device_id={"tensor": toward(direction, distance)}, device_id_type=pl.DeviceIdType.MESH,
        )

    def shrink_parts(matches):
        for b in range(blocks):
            factor = chosen(every_a, cached_a, b, *matches[b])
            part = lax.dot_general(
                acts[pl.ds(b * TILE, TILE)], factor, (((1,), (1,)), ((), ())), preferred_element_type=F32
            )
            for q in range(TILE // piece):
                upper = part[q * piece : q * piece + piece // 2]
                lower = part[q * piece + piece // 2 : (q + 1) * piece]
                part_out[b * (TILE // piece) + q] = jnp.concatenate([upper, lower], axis=1).astype(BF16)
        for kind in (THIRD, FOURTH, ADJACENT):
            for direction in range(2):
                part_copy(kind, direction).start()

    def shrink_merge():
        for direction in range(2):
            part_copy(THIRD, direction).wait_recv()
            part_copy(FOURTH, direction).wait_recv()
            value = part_out[toward(direction, 2)].astype(F32) + part_in[THIRD, direction].astype(F32)
            spot = half_of(direction)
            rest = half_of(1 - direction)
            share = value[direction * slice_half : (direction + 1) * slice_half]
            merged[direction, spot] = (share + part_in[FOURTH, direction, spot].astype(F32)).astype(BF16)
            merged[direction, rest] = value[(1 - direction) * slice_half : (2 - direction) * slice_half].astype(BF16)
            part_copy(MERGED, direction).start()

    def shrink_sum():
        value = part_out[z].astype(F32)
        for kind in (ADJACENT, MERGED):
            for direction in range(2):
                part_copy(kind, direction).wait_recv()
                value = value + part_in[kind, direction].astype(F32)
        shrunk[0] = value.astype(BF16)
        for kind in (1, 0):
            for direction in range(2):
                shrunk_copy(kind, direction).start()

    def shrink_relay():
        for direction in range(2):
            shrunk_copy(1, direction).wait_recv()
            shrunk_copy(3, direction).start()
            shrunk_copy(2, direction).start()

    def expand(matches):
        for kind in (0, 2, 3):
            for direction in range(2):
                shrunk_copy(kind, direction).wait_recv()
        for b in range(blocks):
            factor = chosen(every_b, cached_b, b, *matches[b])
            lines = []
            for q in range(TILE // piece):
                packed = shrunk[(z + Z - b * (TILE // piece) - q) % Z].astype(F32)
                lines += [packed[:, :rank], packed[:, rank:]]
            lines = jnp.concatenate(lines, axis=0).astype(BF16)
            spot = pl.ds(b * TILE, TILE)
            total[spot] = total[spot] + adapter_scale * dot(lines, factor)

    def own_base():
        weight_load(0).wait()
        for i in range(rows // TILE):
            spot = pl.ds(i * TILE, TILE)
            total[spot] = dot(acts[spot], weight[0])

    def add_short():
        for direction, tile in ways:
            ring_copy(direction, LAST_SHORT, tile).wait_recv()
            spot = lines(direction, False, tile)
            total[spot] = total[spot] + incoming[direction, LAST_SHORT, pl.ds(tile * TILE, TILE)].astype(F32)

    def finish():
        size = TILE // PARTS
        for tile in range(tiles):
            for part in range(PARTS):
                for direction in range(2):
                    ring_copy(direction, LAST_LONG, tile, part, PARTS).wait_recv()
                    side = direction * half
                    spot = pl.ds(side + tile * TILE + part * size, size)
                    got = incoming[direction, LAST_LONG, pl.ds(tile * TILE + part * size, size)]
                    result[spot] = (total[spot] + got.astype(F32)).astype(BF16)

    def drain_gather(g):
        for kind in range(8):
            for j, direction in both:
                gather_copy(g, j, kind, direction).wait_send()
        for number in range(4):
            for j in range(2):
                across_copy(g, j, number).wait_send()

    def drain_ring(*slots):
        for slot in slots:
            for direction, tile in ways:
                copies = copies_of(slot, direction, tile)
                if slot == 0 and tile == tiles - 1:
                    copies[0].wait_send()
                    pl.when(z != SHIFTED[direction])(copies[1].wait_send)
                    pl.when(z == SHIFTED[1 - direction])(strip_other(direction).wait_send)
                    continue
                for copy in copies:
                    copy.wait_send()

    weight_load(4).wait()
    loads[0].wait()
    for direction in range(2):
        ring_piece(0, direction, 0)
    pl.semaphore_wait(barrier, 7)
    for direction in range(2):
        ring_send_piece(0, direction, 0)
    for direction in range(2):
        for tile in range(1, tiles):
            ring_piece(0, direction, tile)
            ring_send_piece(0, direction, tile)
    strips_away()
    gather_0(0)
    for i in (3, 5, 2, 6, 1, 7, 0):
        weight_load(i).start()
    for j in range(2):
        fresh_loads[1][j].start()
    for load in loads[1:]:
        load.start()
    ring_step(1)
    own_base()
    for load in loads[1:]:
        load.wait()
    matches = [match(b) for b in range(blocks)]
    gather_1(0)
    ring_step(2)
    strips_on()
    gather_2(0)
    gather_3(0)
    ring_step(3)
    gather_4(0)
    gather_0(1)
    ring_step(4)
    gather_5(0)
    gather_1(1)
    gather_6(0)
    shrink_parts(matches)
    gather_2(1)
    weight_load(1).wait()
    weight_load(7).wait()
    ring_tile(5, 0)
    ring_tile(5, 1, False)
    shrink_merge()
    ring_out(5, 1)
    gather_3(1)
    gather_4(1)
    ring_tile(6, 0, False)
    shrink_sum()
    ring_out(6, 0)
    ring_tile(6, 1, False)
    for direction in range(2):
        copies_of(6, direction, 1)[0].start()
    gather_5(1)
    shrink_relay()
    for direction in range(2):
        copies_of(6, direction, 1)[1].start()
    gather_6(1)
    add_short()
    drain_gather(0)
    drain_gather(1)
    drain_ring(0, 1, 2, 3, 4, 5)
    expand(matches)
    for kind in range(4):
        for direction in range(2):
            part_copy(kind, direction).wait_send()
            shrunk_copy(kind, direction).wait_send()
    finish()
    drain_ring(6)


def shards(acts, weight, block_ids, cached_a, cached_b, renewed_module_numbers, fresh_a, renewed_second_matrices):
    rows, depth = acts.shape
    width = cached_b.shape[2]
    blocks, rank = cached_b.shape[0], cached_b.shape[1]
    tiles = rows // 2 // TILE
    slots = len(SLOTS)
    dma = pltpu.SemaphoreType.DMA
    return pl.pallas_call(
        kernel,
        out_shape=pltpu.VMEM((rows, width), BF16),
        in_specs=[pl.BlockSpec(memory_space=pl.ANY)] * 8,
        out_specs=pl.BlockSpec(memory_space=pltpu.VMEM),
        scratch_shapes=[
            pltpu.VMEM((rows, depth), BF16),
            pltpu.VMEM((Z, depth, width), BF16),
            pltpu.SMEM(block_ids.shape, jnp.int32),
            pltpu.SMEM(renewed_module_numbers.shape, jnp.int32),
            pltpu.VMEM((blocks, rank, depth), BF16),
            pltpu.VMEM((blocks, rank, width), BF16),
            pltpu.VMEM((2 * 2 * SIDE * SIDE, rank, depth), BF16),
            pltpu.VMEM((2 * 2 * SIDE * SIDE, rank, width), BF16),
            pltpu.VMEM((2, slots, rows // 2, width), BF16),
            pltpu.VMEM((2, slots, rows // 2, width), BF16),
            pltpu.VMEM((2, TILE // PARTS, width), BF16),
            pltpu.VMEM((rows, width), F32),
            pltpu.VMEM((Z, rows // Z // 2, 2 * rank), BF16),
            pltpu.VMEM((4, 2, rows // Z // 2, 2 * rank), BF16),
            pltpu.VMEM((2, rows // Z // 2, 2 * rank), BF16),
            pltpu.VMEM((Z, rows // Z // 2, 2 * rank), BF16),
            dma((5,)),
            dma((Z,)),
            dma((2, 2)),
            dma((2, slots, tiles * PARTS)),
            dma((2, slots, tiles * PARTS)),
            dma((2,)),
            dma((2,)),
            dma((2, 2, 20)),
            dma((2, 2, 20)),
            dma((4, 2)),
            dma((4, 2)),
            dma((4, 2)),
            dma((4, 2)),
        ],
        compiler_params=pltpu.CompilerParams(
            collective_id=0, has_side_effects=True, vmem_limit_bytes=60 * 1024 * 1024
        ),
    )(
        acts, weight, block_ids, jnp.swapaxes(cached_a, 1, 2), cached_b,
        renewed_module_numbers, jnp.swapaxes(fresh_a, 1, 2), renewed_second_matrices,
    )


def solution(mesh):
    return jax.shard_map(
        shards,
        mesh=mesh,
        in_specs=(
            P("dp", "tensor"),
            P("tensor", None),
            P("dp"),
            P("dp", "tensor", None),
            P("dp", None, "tensor"),
            P(),
            P("dp", "tensor", None),
            P("dp", None, "tensor"),
        ),
        out_specs=P("dp", "tensor"),
        check_vma=False,
    )
```

```python
import jax
import jax.numpy as jnp
from jax import lax
from jax.experimental import pallas as pl
from jax.experimental.pallas import tpu as pltpu
from jax.sharding import PartitionSpec as P

adapter_scale = 2.0
Z = 8
SIDE = 4
TILE = 128
PARTS = 2
SHIFTED = (7, 4)
BF16 = jnp.bfloat16
F32 = jnp.float32

SLOTS = (
    (True, 0, None),
    (False, 1, None),
    (True, 1, 0),
    (False, 2, 1),
    (True, 2, 2),
    (False, 3, 3),
    (True, 3, 4),
)
LAST_LONG, LAST_SHORT = 6, 5

FIRST, SECOND, FIRST_FAR, SECOND_PAIR, SECOND_FAR, OWN_ON, PAIR_ON, FAR_ON = range(8)
ROWS_ACROSS = 16


def dot(a, b):
    return jnp.dot(a, b, preferred_element_type=F32)


def kernel(
    acts_hbm, weight_hbm, ids_hbm, cached_a_hbm, cached_b_hbm, renewed_hbm, fresh_a_hbm, fresh_b_hbm,
    result,
    acts, weight, ids, renewed, cached_a, cached_b, every_a, every_b,
    outgoing, incoming, strip_in, total, part_out, part_in, merged, shrunk, factor_b,
    load_sem, weight_sem, fresh_sem,
    ring_send, ring_recv, strip_send, strip_recv, gather_send, gather_recv, part_send, part_recv, shrunk_send, shrunk_recv,
):
    z = lax.axis_index("tensor")
    dp = lax.axis_index("dp")
    core = dp % 2
    x = (dp // 2) % SIDE
    y = dp // (2 * SIDE)
    depth, width = weight.shape[1], weight.shape[2]
    blocks = ids_hbm.shape[0]
    rows = acts.shape[0]
    half = rows // 2
    tiles = half // TILE
    rank = cached_a.shape[1]

    def at_xy(px, py, pc):
        return {"dp": (py * SIDE + px) * 2 + pc}

    def along(axis, step):
        if axis == 0:
            return at_xy((x + step + SIDE) % SIDE, y, core)
        return at_xy(x, (y + step + SIDE) % SIDE, core)

    sibling = at_xy(x, y, 1 - core)

    def weight_load(i):
        column = pl.multiple_of((z + i) % Z * width, 128)
        return pltpu.make_async_copy(weight_hbm.at[:, pl.ds(column, width)], weight.at[i], weight_sem.at[i])

    loads = [
        pltpu.make_async_copy(acts_hbm, acts, load_sem.at[0]),
        pltpu.make_async_copy(cached_a_hbm, cached_a, load_sem.at[1]),
        pltpu.make_async_copy(cached_b_hbm, cached_b, load_sem.at[2]),
        pltpu.make_async_copy(ids_hbm, ids, load_sem.at[3]),
        pltpu.make_async_copy(renewed_hbm, renewed, load_sem.at[4]),
    ]
    mine = (
        (core * SIDE + y) * SIDE + (x % 2) * 2 + x // 2,
        ((2 + core) * SIDE + x) * SIDE + (y % 2) * 2 + y // 2,
    )
    gathers = ((every_a, fresh_a_hbm), (every_b, fresh_b_hbm))
    fresh_loads = [
        [pltpu.make_async_copy(source.at[j], held.at[mine[j]], fresh_sem.at[g, j]) for j in range(2)]
        for g, (held, source) in enumerate(gathers)
    ]

    barrier = pltpu.get_barrier_semaphore()
    for i in (1, Z - 1):
        pl.semaphore_signal(barrier, inc=1, device_id={"tensor": (z + i) % Z}, device_id_type=pl.DeviceIdType.MESH)
    for axis in range(2):
        for step in (1, -1):
            pl.semaphore_signal(barrier, inc=1, device_id=along(axis, step), device_id_type=pl.DeviceIdType.MESH)
    pl.semaphore_signal(barrier, inc=1, device_id=sibling, device_id_type=pl.DeviceIdType.MESH)

    weight_load(4).start()
    loads[0].start()
    for j in range(2):
        fresh_loads[0][j].start()

    def ring_copy(direction, slot, tile, part=0, parts=1):
        spot = pl.ds(tile * TILE + part * (TILE // parts), TILE // parts)
        return pltpu.make_async_remote_copy(
            src_ref=outgoing.at[direction, slot, spot],
            dst_ref=incoming.at[direction, slot, spot],
            send_sem=ring_send.at[direction, slot, tile * PARTS + part],
            recv_sem=ring_recv.at[direction, slot, tile * PARTS + part],
            device_id={"tensor": (z + 1 - 2 * direction + Z) % Z},
            device_id_type=pl.DeviceIdType.MESH,
        )

    ways = [(direction, tile) for tile in range(tiles) for direction in range(2)]

    def lines(direction, is_long, tile):
        side = direction if is_long else 1 - direction
        return pl.ds(side * half + tile * TILE, TILE)

    strip = pl.ds(half - TILE // PARTS, TILE // PARTS)

    def parts_of(slot, tile):
        return PARTS if slot == LAST_LONG or (slot < 2 and tile == tiles - 1) else 1

    def copies_of(slot, direction, tile):
        parts = parts_of(slot, tile)
        return [ring_copy(direction, slot, tile, part, parts) for part in range(parts)]

    def strip_other(direction):
        return pltpu.make_async_remote_copy(
            src_ref=outgoing.at[1 - direction, 0, strip],
            dst_ref=strip_in.at[direction],
            send_sem=strip_send.at[direction],
            recv_sem=strip_recv.at[direction],
            device_id={"tensor": (z + 1 - 2 * direction + Z) % Z},
            device_id_type=pl.DeviceIdType.MESH,
        )

    def before_me(direction):
        return (z - 1 + 2 * direction + Z) % Z

    def ring_piece(slot, direction, tile):
        is_long, step, before = SLOTS[slot]
        spot = pl.ds(tile * TILE, TILE)
        term = dot(acts[lines(direction, is_long, tile)], weight[4 - step + 2 * step * direction])
        if before == 0 and tile == tiles - 1:
            first = pl.ds(tile * TILE, TILE // PARTS)
            kept, ends = copies_of(0, direction, tile)
            kept.wait_recv()
            upper = term[: TILE // PARTS] + incoming[direction, 0, first].astype(F32)
            outgoing[direction, slot, first] = upper.astype(BF16)
            outgoing[direction, slot, strip] = term[TILE // PARTS :].astype(BF16)

            @pl.when(before_me(direction) != SHIFTED[direction])
            def _():
                ends.wait_recv()
                lower = outgoing[direction, slot, strip].astype(F32) + incoming[direction, 0, strip].astype(F32)
                outgoing[direction, slot, strip] = lower.astype(BF16)

            return
        if before is not None:
            for copy in copies_of(before, direction, tile):
                copy.wait_recv()
            term = term + incoming[direction, before, spot].astype(F32)
        outgoing[direction, slot, spot] = term.astype(BF16)

    def ring_send_piece(slot, direction, tile):
        copies = copies_of(slot, direction, tile)
        if slot < 2 and tile == tiles - 1:
            copies[0].start()
            if slot == 0:
                pl.when(z != SHIFTED[direction])(copies[1].start)
            return
        for copy in copies:
            copy.start()

    def strips_away():
        for direction in range(2):
            pl.when(z == SHIFTED[1 - direction])(strip_other(direction).start)

    def strips_on():
        for direction in range(2):

            @pl.when(before_me(direction) == SHIFTED[1 - direction])
            def _():
                strip_other(direction).wait_recv()
                value = outgoing[direction, 1, strip].astype(F32) + strip_in[direction].astype(F32)
                outgoing[direction, 1, strip] = value.astype(BF16)

            copies_of(1, direction, tiles - 1)[1].start()

    def ring_step(slot):
        is_long, step, _ = SLOTS[slot]
        if not is_long:
            weight_load(4 - step).wait()
            weight_load(4 + step).wait()
        for tile in range(tiles):
            ring_tile(slot, tile)

    def ring_tile(slot, tile, send=True):
        for direction in range(2):
            ring_piece(slot, direction, tile)
            if send:
                ring_send_piece(slot, direction, tile)

    def ring_out(slot, tile):
        for direction in range(2):
            ring_send_piece(slot, direction, tile)

    def line_of(j, second, of_core):
        return ((j * 2 + of_core) * SIDE + second) * SIDE

    def across_line(first):
        return (first % 2) * 2 + first // 2

    def gather_copy(g, j, kind, direction=0, incoming_side=False):
        held = gathers[g][0]
        first, second = (x, y) if j == 0 else (y, x)
        first_axis, second_axis = (0, 1) if j == 0 else (1, 0)
        sign = 1 - 2 * direction
        back = -sign if incoming_side else 0
        here = across_line(first)
        pair = (1 - first % 2) * 2
        far = across_line((first + 2) % SIDE)
        part = pl.ds(direction * (rank // 2), rank // 2)

        def line(step):
            return line_of(j, (second + step + SIDE) % SIDE, core)

        axis = second_axis
        if kind == FIRST:
            axis = first_axis
            ref = held.at[line(0) + across_line((first + back + SIDE) % SIDE)]
        elif kind == FIRST_FAR:
            axis = first_axis
            ref = held.at[line(0) + across_line((first + back - sign + SIDE) % SIDE), part]
        elif kind == SECOND:
            ref = held.at[line(back) + here]
        elif kind == SECOND_PAIR:
            ref = held.at[pl.ds(line(back) + pair, 2)]
        elif kind == SECOND_FAR:
            ref = held.at[line(back) + far]
        elif kind == OWN_ON:
            ref = held.at[line(back - sign) + here, part]
        elif kind == PAIR_ON:
            ref = held.at[line(back - sign) + pair + direction]
        else:
            ref = held.at[line(back - sign) + far, part]
        number = 2 * kind + direction
        return pltpu.make_async_remote_copy(
            src_ref=ref, dst_ref=ref,
            send_sem=gather_send.at[g, j, number], recv_sem=gather_recv.at[g, j, number],
            device_id=along(axis, sign), device_id_type=pl.DeviceIdType.MESH,
        )

    def across_copy(g, j, number, incoming_side=False):
        held = gathers[g][0]
        second = y if j == 0 else x
        moved = (second + (0, -1, 1, 2)[number] + SIDE) % SIDE
        ref = held.at[pl.ds(line_of(j, moved, 1 - core if incoming_side else core), SIDE)]
        return pltpu.make_async_remote_copy(
            src_ref=ref, dst_ref=ref,
            send_sem=gather_send.at[g, j, ROWS_ACROSS + number], recv_sem=gather_recv.at[g, j, ROWS_ACROSS + number],
            device_id=sibling, device_id_type=pl.DeviceIdType.MESH,
        )

    both = [(j, direction) for j in range(2) for direction in range(2)]

    def send_all(g, *kinds):
        for kind in kinds:
            for j, direction in both:
                gather_copy(g, j, kind, direction).start()

    def take_all(g, *kinds):
        for kind in kinds:
            for j, direction in both:
                gather_copy(g, j, kind, direction, True).wait_recv()

    def send_across(g, *numbers):
        for number in numbers:
            for j in range(2):
                across_copy(g, j, number).start()

    def gather_0(g):
        for j in range(2):
            fresh_loads[g][j].wait()
        send_all(g, FIRST, SECOND)

    def gather_1(g):
        take_all(g, FIRST)
        send_all(g, FIRST_FAR, SECOND_PAIR)

    def gather_2(g):
        take_all(g, FIRST_FAR)
        send_all(g, SECOND_FAR)
        take_all(g, SECOND)
        send_all(g, OWN_ON)
        send_across(g, 0)

    def gather_3(g):
        take_all(g, SECOND_PAIR)
        send_all(g, PAIR_ON)

    def gather_4(g):
        take_all(g, SECOND_FAR)
        send_all(g, FAR_ON)
        send_across(g, 1, 2)

    def gather_5(g):
        take_all(g, OWN_ON, PAIR_ON, FAR_ON)
        send_across(g, 3)

    def gather_6(g):
        for number in range(4):
            for j in range(2):
                across_copy(g, j, number, True).wait_recv()

    def match(b):
        def body(i, carry):
            found, where = carry
            hit = renewed[i] == ids[b]
            return jnp.where(hit, 1, found), jnp.where(hit, i, where)

        return lax.fori_loop(0, renewed_hbm.shape[0], body, (jnp.int32(0), jnp.int32(0)))

    def chosen(held, cached, b, found, where):
        j, of_core, px, py = where % 2, (where // 2) % 2, (where // 4) % SIDE, where // 16
        second, first = jnp.where(j == 0, py, px), jnp.where(j == 0, px, py)
        return jnp.where(found > 0, held[line_of(j, second, of_core) + across_line(first)], cached[b])

    piece = rows // Z

    slice_half = piece // 4
    ADJACENT, THIRD, FOURTH, MERGED = range(4)

    def toward(direction, distance):
        return (z + distance * (1 - 2 * direction) + Z) % Z

    def half_of(direction):
        return pl.ds(direction * slice_half, slice_half)

    def part_copy(kind, direction):
        if kind == ADJACENT:
            src, distance = part_out.at[toward(direction, 1)], 1
        elif kind == THIRD:
            src, distance = part_out.at[toward(direction, 3)], 1
        elif kind == FOURTH:
            src, distance = part_out.at[toward(direction, 4), half_of(direction)], 2
        else:
            src, distance = merged.at[direction], 2
        dst = part_in.at[kind, direction]
        return pltpu.make_async_remote_copy(
            src_ref=src, dst_ref=dst.at[half_of(direction)] if kind == FOURTH else dst,
            send_sem=part_send.at[kind, direction], recv_sem=part_recv.at[kind, direction],
            device_id={"tensor": toward(direction, distance)}, device_id_type=pl.DeviceIdType.MESH,
        )

    def shrunk_copy(kind, direction):
        if kind < 2:
            src, dst, distance = shrunk.at[0], shrunk.at[(Z - 1 - kind) if direction else 1 + kind], 1 + kind
        elif kind == 2:
            src, dst, distance = shrunk.at[6 if direction else 2], shrunk.at[5 if direction else 3], 1
        else:
            spot = half_of(direction)
            src, dst, distance = shrunk.at[6 if direction else 2, spot], shrunk.at[4, spot], 2
        return pltpu.make_async_remote_copy(
            src_ref=src, dst_ref=dst,
            send_sem=shrunk_send.at[kind, direction], recv_sem=shrunk_recv.at[kind, direction],
            device_id={"tensor": toward(direction, distance)}, device_id_type=pl.DeviceIdType.MESH,
        )

    def shrink_parts(matches):
        for b in range(blocks):
            factor = chosen(every_a, cached_a, b, *matches[b])
            part = lax.dot_general(
                acts[pl.ds(b * TILE, TILE)], factor, (((1,), (1,)), ((), ())), preferred_element_type=F32
            )
            for q in range(TILE // piece):
                upper = part[q * piece : q * piece + piece // 2]
                lower = part[q * piece + piece // 2 : (q + 1) * piece]
                part_out[b * (TILE // piece) + q] = jnp.concatenate([upper, lower], axis=1).astype(BF16)
        for kind in (THIRD, FOURTH, ADJACENT):
            for direction in range(2):
                part_copy(kind, direction).start()

    def shrink_merge():
        for direction in range(2):
            part_copy(THIRD, direction).wait_recv()
            part_copy(FOURTH, direction).wait_recv()
            value = part_out[toward(direction, 2)].astype(F32) + part_in[THIRD, direction].astype(F32)
            spot = half_of(direction)
            rest = half_of(1 - direction)
            share = value[direction * slice_half : (direction + 1) * slice_half]
            merged[direction, spot] = (share + part_in[FOURTH, direction, spot].astype(F32)).astype(BF16)
            merged[direction, rest] = value[(1 - direction) * slice_half : (2 - direction) * slice_half].astype(BF16)
            part_copy(MERGED, direction).start()

    def shrink_sum():
        value = part_out[z].astype(F32)
        for kind in (ADJACENT, MERGED):
            for direction in range(2):
                part_copy(kind, direction).wait_recv()
                value = value + part_in[kind, direction].astype(F32)
        shrunk[0] = value.astype(BF16)
        for kind in (1, 0):
            for direction in range(2):
                shrunk_copy(kind, direction).start()

    def shrink_relay():
        for direction in range(2):
            shrunk_copy(1, direction).wait_recv()
            shrunk_copy(3, direction).start()
            shrunk_copy(2, direction).start()

    def choose_b(matches):
        for b in range(blocks):
            factor_b[b] = chosen(every_b, cached_b, b, *matches[b])

    def expand(*slices):
        for i in slices:
            q = (z + Z - i) % Z
            packed = shrunk[i].astype(F32)
            lines = jnp.concatenate([packed[:, :rank], packed[:, rank:]], axis=0).astype(BF16)
            spot = pl.ds(pl.multiple_of(q * piece, piece), piece)
            total[spot] = total[spot] + adapter_scale * dot(lines, factor_b[q // (TILE // piece)])

    def take_shrunk(*kinds):
        for kind in kinds:
            for direction in range(2):
                shrunk_copy(kind, direction).wait_recv()

    def own_base():
        weight_load(0).wait()
        for i in range(rows // TILE):
            spot = pl.ds(i * TILE, TILE)
            total[spot] = dot(acts[spot], weight[0])

    def add_short():
        for direction, tile in ways:
            ring_copy(direction, LAST_SHORT, tile).wait_recv()
            spot = lines(direction, False, tile)
            total[spot] = total[spot] + incoming[direction, LAST_SHORT, pl.ds(tile * TILE, TILE)].astype(F32)

    def finish():
        size = TILE // PARTS
        for tile in range(tiles):
            for part in range(PARTS):
                for direction in range(2):
                    ring_copy(direction, LAST_LONG, tile, part, PARTS).wait_recv()
                    side = direction * half
                    spot = pl.ds(side + tile * TILE + part * size, size)
                    got = incoming[direction, LAST_LONG, pl.ds(tile * TILE + part * size, size)]
                    result[spot] = (total[spot] + got.astype(F32)).astype(BF16)

    def drain_gather(g):
        for kind in range(8):
            for j, direction in both:
                gather_copy(g, j, kind, direction).wait_send()
        for number in range(4):
            for j in range(2):
                across_copy(g, j, number).wait_send()

    def drain_ring(*slots):
        for slot in slots:
            for direction, tile in ways:
                copies = copies_of(slot, direction, tile)
                if slot == 0 and tile == tiles - 1:
                    copies[0].wait_send()
                    pl.when(z != SHIFTED[direction])(copies[1].wait_send)
                    pl.when(z == SHIFTED[1 - direction])(strip_other(direction).wait_send)
                    continue
                for copy in copies:
                    copy.wait_send()

    weight_load(4).wait()
    loads[0].wait()
    for direction in range(2):
        ring_piece(0, direction, 0)
    pl.semaphore_wait(barrier, 7)
    for direction in range(2):
        ring_send_piece(0, direction, 0)
    for direction in range(2):
        for tile in range(1, tiles):
            ring_piece(0, direction, tile)
            ring_send_piece(0, direction, tile)
    strips_away()
    gather_0(0)
    for i in (3, 5, 2, 6, 1, 7, 0):
        weight_load(i).start()
    for j in range(2):
        fresh_loads[1][j].start()
    for load in loads[1:]:
        load.start()
    ring_step(1)
    own_base()
    for load in loads[1:]:
        load.wait()
    matches = [match(b) for b in range(blocks)]
    gather_1(0)
    ring_step(2)
    strips_on()
    gather_2(0)
    gather_3(0)
    ring_step(3)
    gather_4(0)
    gather_0(1)
    ring_step(4)
    gather_5(0)
    gather_1(1)
    gather_6(0)
    shrink_parts(matches)
    gather_2(1)
    weight_load(1).wait()
    weight_load(7).wait()
    ring_tile(5, 0)
    ring_tile(5, 1, False)
    shrink_merge()
    ring_out(5, 1)
    gather_3(1)
    gather_4(1)
    ring_tile(6, 0, False)
    shrink_sum()
    ring_out(6, 0)
    ring_tile(6, 1, False)
    gather_5(1)
    shrink_relay()
    ring_out(6, 1)
    gather_6(1)
    choose_b(matches)
    take_shrunk(0)
    expand(0, 1, 7, 2, 6)
    add_short()
    drain_gather(0)
    drain_gather(1)
    drain_ring(0, 1, 2, 3, 4, 5)
    take_shrunk(2, 3)
    expand(3, 5, 4)
    for kind in range(4):
        for direction in range(2):
            part_copy(kind, direction).wait_send()
            shrunk_copy(kind, direction).wait_send()
    finish()
    drain_ring(6)


def shards(acts, weight, block_ids, cached_a, cached_b, renewed_module_numbers, fresh_a, renewed_second_matrices):
    rows, depth = acts.shape
    width = cached_b.shape[2]
    blocks, rank = cached_b.shape[0], cached_b.shape[1]
    tiles = rows // 2 // TILE
    slots = len(SLOTS)
    dma = pltpu.SemaphoreType.DMA
    return pl.pallas_call(
        kernel,
        out_shape=pltpu.VMEM((rows, width), BF16),
        in_specs=[pl.BlockSpec(memory_space=pl.ANY)] * 8,
        out_specs=pl.BlockSpec(memory_space=pltpu.VMEM),
        scratch_shapes=[
            pltpu.VMEM((rows, depth), BF16),
            pltpu.VMEM((Z, depth, width), BF16),
            pltpu.SMEM(block_ids.shape, jnp.int32),
            pltpu.SMEM(renewed_module_numbers.shape, jnp.int32),
            pltpu.VMEM((blocks, rank, depth), BF16),
            pltpu.VMEM((blocks, rank, width), BF16),
            pltpu.VMEM((2 * 2 * SIDE * SIDE, rank, depth), BF16),
            pltpu.VMEM((2 * 2 * SIDE * SIDE, rank, width), BF16),
            pltpu.VMEM((2, slots, rows // 2, width), BF16),
            pltpu.VMEM((2, slots, rows // 2, width), BF16),
            pltpu.VMEM((2, TILE // PARTS, width), BF16),
            pltpu.VMEM((rows, width), F32),
            pltpu.VMEM((Z, rows // Z // 2, 2 * rank), BF16),
            pltpu.VMEM((4, 2, rows // Z // 2, 2 * rank), BF16),
            pltpu.VMEM((2, rows // Z // 2, 2 * rank), BF16),
            pltpu.VMEM((Z, rows // Z // 2, 2 * rank), BF16),
            pltpu.VMEM((blocks, rank, width), BF16),
            dma((5,)),
            dma((Z,)),
            dma((2, 2)),
            dma((2, slots, tiles * PARTS)),
            dma((2, slots, tiles * PARTS)),
            dma((2,)),
            dma((2,)),
            dma((2, 2, 20)),
            dma((2, 2, 20)),
            dma((4, 2)),
            dma((4, 2)),
            dma((4, 2)),
            dma((4, 2)),
        ],
        compiler_params=pltpu.CompilerParams(
            collective_id=0, has_side_effects=True, vmem_limit_bytes=60 * 1024 * 1024
        ),
    )(
        acts, weight, block_ids, jnp.swapaxes(cached_a, 1, 2), cached_b,
        renewed_module_numbers, jnp.swapaxes(fresh_a, 1, 2), renewed_second_matrices,
    )


def solution(mesh):
    return jax.shard_map(
        shards,
        mesh=mesh,
        in_specs=(
            P("dp", "tensor"),
            P("tensor", None),
            P("dp"),
            P("dp", "tensor", None),
            P("dp", None, "tensor"),
            P(),
            P("dp", "tensor", None),
            P("dp", None, "tensor"),
        ),
        out_specs=P("dp", "tensor"),
        check_vma=False,
    )
```
